32 devices in a mesh: segment: 2 (over y), seq: 4 (over x, core), tp: 4 (over z).
Axes of the slice: x: 2, y: 2, z: 4, core: 2. Of those that a mesh axis runs over, the one named last changes fastest.
Arguments:
- queries: bfloat16 [2, 768, 4096], P('segment', 'seq', 'tp'), may hold values from -64 to 64
- nb_keys: bfloat16 [2, 12, 256, 4096], P('segment', 'seq', None, 'tp'), may hold values from -24 to 24
- nb_values: bfloat16 [2, 12, 256, 4096], P('segment', 'seq', None, 'tp'), may hold values from -6 to 6
- nb_lengths: int32 [2, 12, 2], P('segment', 'seq'), may hold values from 1 to 128
- slot_stretch: int32 [2, 12], P('segment', 'seq'), may hold values from 0 to 11, as said below
- out_weight: bfloat16 [2, 4096, 4096], P('segment', 'tp', 'seq'), may hold values from -0.09375 to 0.09375
- residual: bfloat16 [2, 768, 4096], P('segment', 'seq', 'tp'), may hold values from -6 to 6
Outputs:
- mixed: bfloat16 [2, 768, 4096], P('segment', 'seq', 'tp')
The draws below stay inside these ranges and needn't reach their ends.
Inputs may be any that keep to these rules, and one draw needn't show every extreme that they name: Each row slot_stretch[e] is a permutation of the 12 stretches. The 3 stretches of one decoder device (stretches i * 3 to i * 3 + 2) are served by slots on 3 different encoder devices, so one decoder device sends at most one stretch to one encoder device.
All inputs are finite; a program needn't handle non-finite values.
Results may differ from the reference program's by a relative error of at most 0.0034.
Values may be sent and summed in bfloat16 or wider, within the bound.
A program may use at most 64 MiB of HBM per device.

```python
import math
import jax
import jax.numpy as jnp
from jax import lax

D = 4096
HEADS = 32
HD = 128
STRETCH = 64
NR = 128
KN = 2
CH_DEV = 3
HA = 4096
NCHUNK = 12
TOKENS = 768
N_SEGMENT = 2
N_SEQ = 4


def draw_queries(key, part):
    key = jax.random.fold_in(key, 5)
    first = jax.random.fold_in(key, 0)
    base = jax.random.normal(first, (N_SEGMENT, TOKENS, HEADS, HD), jnp.float32)
    return jnp.clip(base, -64.0, 64.0).reshape(N_SEGMENT, TOKENS, HEADS * HD).astype(jnp.bfloat16)


def draw_nb_keys(key, part):
    key = jax.random.fold_in(key, 7)
    first = jax.random.fold_in(key, 0)
    base = jax.random.normal(first, (N_SEGMENT, NCHUNK, KN * NR, HEADS, HD), jnp.float32)
    return jnp.clip(base, -24.0, 24.0).reshape(N_SEGMENT, NCHUNK, KN * NR, HEADS * HD).astype(jnp.bfloat16)


def draw_slot_stretch(key, part):
    key = jax.random.fold_in(key, 9)

    def one_section(section_key):
        key_a, key_b, key_c, key_d = jax.random.split(section_key, 4)
        spread = jax.random.permutation(key_a, N_SEQ)
        order = jax.random.permutation(key_b, N_SEQ)
        offsets = jax.random.permutation(key_c, N_SEQ)[:CH_DEV]
        places = jax.random.permutation(key_d, CH_DEV)
        owners = jnp.arange(N_SEQ, dtype=jnp.int32)[:, None]
        within = jnp.arange(CH_DEV, dtype=jnp.int32)[None, :]
        holders = spread[(order[owners] + offsets[within]) % N_SEQ]
        slots = holders * CH_DEV + places[within]
        stretches = owners * CH_DEV + within
        return jnp.zeros((NCHUNK,), jnp.int32).at[slots.reshape(-1)].set(stretches.reshape(-1))
    return jax.vmap(one_section)(jax.random.split(key, N_SEGMENT))


def plant(values, stream_key, least, largest):
    extent = values.shape
    place = [jax.random.randint(jax.random.fold_in(stream_key, axis), (), 0, extent[axis]) for axis in range(len(extent))]
    values = values.at[tuple(place)].set(least)
    longest = extent.index(max(extent))
    place[longest] = (place[longest] + 1) % extent[longest]
    return values.at[tuple(place)].set(largest)


def block_scale(own_key, dims, cuts, low, largest):
    gain = 1.0
    for dim, blocks in cuts:
        draws = jax.random.uniform(jax.random.fold_in(jax.random.fold_in(own_key, 6), dim), (blocks,), jnp.float32, low / len(cuts), largest / len(cuts))
        gain = gain * jnp.repeat(jnp.exp(draws), dims[dim] // blocks).reshape((-1,) + (1,) * (len(dims) - 1 - dim))
    return gain


def bell_draw(stream_key, shape, scale, limit, shards=(), held_as=jnp.bfloat16):
    array = scale * jax.random.normal(stream_key, shape, jnp.float32)
    if shards:
        array = array * block_scale(stream_key, shape, shards, -0.22, 0.18)
    return jnp.clip(array, -limit, limit).astype(held_as)


def setup_inputs(seed: int = 0) -> dict:
    seeds = jax.random.split(jax.random.key(seed), 8)
    return {
        "queries": draw_queries(jax.random.fold_in(seeds[7], 71), 0),
        "nb_keys": draw_nb_keys(jax.random.fold_in(seeds[7], 71), 0),
        "nb_values": bell_draw(seeds[2], (N_SEGMENT, NCHUNK, KN * NR, HA), 1.0, 6.0, ((0, 2), (1, 4), (3, 4))),
        "nb_lengths": plant(jax.random.randint(seeds[3], (N_SEGMENT, NCHUNK, KN), 1, NR + 1), jax.random.fold_in(seeds[3], 1), 1, NR).astype(jnp.int32),
        "slot_stretch": draw_slot_stretch(jax.random.fold_in(seeds[7], 71), 0),
        "out_weight": bell_draw(seeds[5], (N_SEGMENT, HA, D), HA ** -0.5, 0.09375, ((0, 2), (1, 4), (2, 4))),
        "residual": bell_draw(seeds[6], (N_SEGMENT, TOKENS, D), 1.0, 6.0, ((0, 2), (1, 4), (2, 4))),
    }


def attend(query_rows, key_rows, value_rows, lengths):
    count, width, feats = query_rows.shape
    span = key_rows.shape[1]
    query_heads = query_rows.reshape(count, width, HEADS, HD).astype(jnp.float32)
    key_heads = key_rows.reshape(count, span, HEADS, HD).astype(jnp.float32)
    value_heads = value_rows.reshape(count, span, HEADS, HD).astype(jnp.float32)
    scores = jnp.einsum('cqhd,clhd->chql', query_heads, key_heads) * (1.0 / math.sqrt(HD))
    position = jnp.arange(span, dtype=jnp.int32)
    limits = jnp.take(lengths, position // NR, axis=1)
    valid = ((position % NR)[None, :] < limits)[:, None, None, :]
    highest = lax.optimization_barrier(jnp.max(jnp.where(valid, scores, -1e+30), axis=-1, keepdims=True))
    expo = jnp.exp(jnp.where(valid, scores - highest, -1e+30))
    weights = (expo / lax.optimization_barrier(jnp.sum(expo, axis=-1, keepdims=True))).astype(jnp.bfloat16)
    mixed = jnp.einsum('chql,clhd->cqhd', weights.astype(jnp.float32), value_heads)
    return mixed.astype(jnp.bfloat16).reshape(count * width, feats)

def reference(queries, nb_keys, nb_values, nb_lengths, slot_stretch, out_weight, residual):
    results = []
    for section in range(N_SEGMENT):
        source = (section - 1) % N_SEGMENT
        inverse = jnp.zeros((NCHUNK,), jnp.int32).at[slot_stretch[source]].set(jnp.arange(NCHUNK, dtype=jnp.int32))
        key_rows = jnp.take(nb_keys[source], inverse, axis=0)
        value_rows = jnp.take(nb_values[source], inverse, axis=0)
        lengths = jnp.take(nb_lengths[source], inverse, axis=0)
        query_rows = queries[section].reshape(NCHUNK, STRETCH, HEADS * HD)
        cca = attend(query_rows, key_rows, value_rows, lengths)
        projected = jnp.dot(cca, out_weight[section], preferred_element_type=jnp.float32)
        results.append((residual[section].astype(jnp.float32) + projected).astype(jnp.bfloat16))
    return jnp.stack(results)
```

```python
import math

import jax
import jax.numpy as jnp
from jax import lax
from jax.sharding import PartitionSpec as P

HD = 128
STRETCH = 64
NR = 128


def shifted(value, axis, by):
    size = lax.axis_size(axis)
    return lax.ppermute(value, axis, [(i, (i + by) % size) for i in range(size)])


def attend(query_rows, key_rows, value_rows, lengths):
    count, width, feats = query_rows.shape
    heads = feats // HD
    span = key_rows.shape[1]
    query_heads = query_rows.reshape(count, width, heads, HD)
    key_heads = key_rows.reshape(count, span, heads, HD)
    value_heads = value_rows.reshape(count, span, heads, HD)
    scores = jnp.einsum(
        "cqhd,clhd->chql", query_heads, key_heads, preferred_element_type=jnp.float32
    ) * (1.0 / math.sqrt(HD))
    position = jnp.arange(span, dtype=jnp.int32)
    limits = jnp.take(lengths, position // NR, axis=1)
    valid = ((position % NR)[None, :] < limits)[:, None, None, :]
    highest = jnp.max(jnp.where(valid, scores, -1e30), axis=-1, keepdims=True)
    expo = jnp.exp(jnp.where(valid, scores - highest, -1e30))
    weights = (expo / jnp.sum(expo, axis=-1, keepdims=True)).astype(jnp.bfloat16)
    mixed = jnp.einsum("chql,clhd->cqhd", weights, value_heads, preferred_element_type=jnp.float32)
    return mixed.astype(jnp.bfloat16).reshape(count, width, feats)


def local(queries, nb_keys, nb_values, nb_lengths, slot_stretch, out_weight, residual):
    count_dev = lax.axis_size("seq")
    seq_index = lax.axis_index("seq")
    per_dev = slot_stretch.shape[1]
    feats = queries.shape[2]
    rows = queries.shape[1]
    total = count_dev * per_dev
    mine = slot_stretch[0]
    lowered = shifted(queries[0].reshape(per_dev, STRETCH, feats), "segment", -1)
    spread = lax.all_gather(lowered, "seq", axis=0, tiled=True)
    picked = jnp.take(spread, mine, axis=0)
    answer = attend(picked, nb_keys[0], nb_values[0], nb_lengths[0])
    table_row = lax.all_gather(shifted(mine, "segment", 1), "seq", axis=0, tiled=True)
    answers = lax.all_gather(shifted(answer, "segment", 1), "seq", axis=0, tiled=True)
    stretch_ids = jnp.arange(total, dtype=jnp.int32)
    matched = table_row[None, :] == stretch_ids[:, None]
    slots = jnp.sum(jnp.where(matched, stretch_ids[None, :], 0), axis=1)
    cca = jnp.take(answers, slots, axis=0).reshape(total * STRETCH, feats)
    partial_out = jnp.dot(cca, out_weight[0], preferred_element_type=jnp.float32)
    blocks = partial_out.astype(jnp.bfloat16).reshape(count_dev, rows, out_weight.shape[2])
    columns = lax.all_to_all(blocks, "seq", split_axis=0, concat_axis=0, tiled=True)
    wide = columns.transpose(1, 0, 2).reshape(rows, -1)
    summed = lax.psum_scatter(wide.astype(jnp.float32), "tp", scatter_dimension=1, tiled=True)
    mixed = (residual[0].astype(jnp.float32) + summed).astype(jnp.bfloat16)
    return mixed[None]


def solution(mesh):
    in_specs = (
        P("segment", "seq", "tp"),
        P("segment", "seq", None, "tp"),
        P("segment", "seq", None, "tp"),
        P("segment", "seq", None),
        P("segment", "seq"),
        P("segment", "tp", "seq"),
        P("segment", "seq", "tp"),
    )
    out_specs = P("segment", "seq", "tp")
    return jax.shard_map(local, mesh=mesh, in_specs=in_specs, out_specs=out_specs, check_vma=False)
```

```python
import functools
import math

import jax
import jax.numpy as jnp
from jax import lax
from jax.experimental import pallas as pl
from jax.experimental.pallas import tpu as pltpu
from jax.sharding import PartitionSpec as P

HD = 128
STRETCH = 64
NR = 128
MESH = pl.DeviceIdType.MESH
F32 = jnp.float32
BF16 = jnp.bfloat16


def hops(count):
    steps, held = [], [0]
    bit = count // 2
    while bit:
        steps.append((bit, tuple(held)))
        held = held + [mask ^ bit for mask in held]
        bit //= 2
    return steps


def kernel(
    n_seg, n_seq, n_tp, per_dev,
    q_hbm, k_hbm, v_hbm, w_hbm, res_hbm, len_ref, slot_ref, table_ref,
    out_ref,
    kbuf, vbuf, wbuf, resbuf, qbuf, abuf, ans, psend, rbuf, upbuf, downbuf, tbuf, tsmem,
    load_sem, qy_send, qy_recv, qx_send, qx_recv, ay_send, ay_recv, ax_send, ax_recv,
    t_send, t_recv, p_send, p_recv, up_send, up_recv, down_send, down_recv,
):
    seg, seq, tp = lax.axis_index("segment"), lax.axis_index("seq"), lax.axis_index("tp")
    before = lax.rem(seg + n_seg - 1, n_seg)
    after = lax.rem(seg + 1, n_seg)
    span = k_hbm.shape[1]
    feats = q_hbm.shape[2]
    width = w_hbm.shape[1]
    ratio = n_seq // n_tp
    heads = feats // HD

    def xor(mask):
        out, bit = seq, 1
        while bit <= mask:
            if mask & bit:
                digit = lax.rem(lax.div(seq, bit), 2)
                out = out + bit - 2 * bit * digit
            bit *= 2
        return out

    partner = [xor(mask) for mask in range(n_seq)]

    loads = [
        pltpu.make_async_copy(src, dst, load_sem.at[i])
        for i, (src, dst) in enumerate(
            [(k_hbm, kbuf), (v_hbm, vbuf), (w_hbm, wbuf), (res_hbm, resbuf)]
        )
    ]

    barrier = pltpu.get_barrier_semaphore()

    def greet(device):
        pl.semaphore_signal(barrier, inc=1, device_id=device, device_id_type=MESH)

    sections = [after] if n_seg == 2 else [before, after]
    for mask in range(n_seq):
        for section in sections:
            greet((section, partner[mask], tp))
        if mask:
            greet((seg, partner[mask], tp))

    @pl.when(tp > 0)
    def _():
        greet((seg, seq, tp - 1))

    @pl.when(tp < n_tp - 1)
    def _():
        greet((seg, seq, tp + 1))

    for load in loads:
        load.start()
    line = jnp.int32(2) - (tp == 0).astype(jnp.int32) - (tp == n_tp - 1).astype(jnp.int32)
    pl.semaphore_wait(barrier, len(sections) * n_seq + n_seq - 1 + line)

    def remote(src, dst, send, recv, device):
        return pltpu.make_async_remote_copy(
            src_ref=src, dst_ref=dst, send_sem=send, recv_sem=recv,
            device_id=device, device_id_type=MESH,
        )

    pending = []

    qy = [
        remote(q_hbm.at[c], qbuf.at[seq * per_dev + c], qy_send.at[c], qy_recv.at[c], (before, seq, tp))
        for c in range(per_dev)
    ]
    for copy in qy:
        copy.start()
    pending += qy

    tables = [
        remote(table_ref, tbuf.at[seq], t_send.at[m], t_recv.at[m], (after, partner[m], tp))
        for m in range(n_seq)
    ]
    for copy in tables:
        copy.start()
    pending += tables

    steps = hops(n_seq)

    def spread(buf, send, recv, c):
        groups, at = [], 0
        for bit, held in steps:
            group = []
            for mask in held:
                place = buf.at[partner[mask] * per_dev + c]
                group.append(
                    remote(place, place, send.at[at, c], recv.at[at, c], (seg, partner[bit], tp))
                )
                at += 1
            groups.append(group)
        return groups

    def relay(first, groups):
        for c in range(per_dev):
            first[c].wait_recv()
            for group in groups[c]:
                group[0].start()
        for level in range(len(steps)):
            for c in range(per_dev):
                for at, copy in enumerate(groups[c][level]):
                    copy.wait_recv()
                    mask = steps[level][0] ^ steps[level][1][at]
                    for later in range(level + 1, len(steps)):
                        groups[c][later][steps[later][1].index(mask)].start()

    q_groups = [spread(qbuf, qx_send, qx_recv, c) for c in range(per_dev)]
    relay(qy, q_groups)
    pending += [copy for groups in q_groups for group in groups for copy in group]

    loads[0].wait()
    loads[1].wait()
    position = lax.broadcasted_iota(jnp.int32, (1, span), 1)
    ay = []
    for k in range(per_dev):
        limit = jnp.zeros((1, span), jnp.int32)
        for j in range(span // NR):
            inside = (position >= j * NR) & (position < (j + 1) * NR)
            limit = jnp.where(inside, j * NR + len_ref[k, j], limit)
        valid = position < limit
        stretch = slot_ref[0, k]
        for h in range(heads):
            cols = pl.ds(h * HD, HD)
            query = qbuf[stretch, :, cols]
            scores = lax.dot_general(
                query, kbuf[k, :, cols], (((1,), (1,)), ((), ())), preferred_element_type=F32
            ) * (1.0 / math.sqrt(HD))
            highest = jnp.max(jnp.where(valid, scores, -1e30), axis=1, keepdims=True)
            expo = jnp.exp(jnp.where(valid, scores - highest, -1e30))
            weights = (expo / jnp.sum(expo, axis=1, keepdims=True)).astype(BF16)
            ans[k, :, cols] = jnp.dot(
                weights, vbuf[k, :, cols], preferred_element_type=F32
            ).astype(BF16)
        copy = remote(
            ans.at[k], abuf.at[seq * per_dev + k], ay_send.at[k], ay_recv.at[k], (after, seq, tp)
        )
        copy.start()
        ay.append(copy)
    pending += ay

    a_groups = [spread(abuf, ax_send, ax_recv, c) for c in range(per_dev)]
    relay(ay, a_groups)
    pending += [copy for groups in a_groups for group in groups for copy in group]

    for copy in tables:
        copy.wait_recv()
    scalars = pltpu.make_async_copy(tbuf, tsmem, load_sem.at[4])
    scalars.start()
    scalars.wait()
    served = [tsmem[g // per_dev, 0, g % per_dev] for g in range(n_seq * per_dev)]

    def slot_of(stretch):
        slot = jnp.int32(0)
        for g, value in enumerate(served):
            slot = jnp.where(value == stretch, jnp.int32(g), slot)
        return slot

    loads[2].wait()
    order = list(range(n_seq - 1, -1, -1))
    if ratio == 1:
        mine = lambda c: rbuf.at[seq, c]
    else:
        lanes = pl.ds(pl.multiple_of(lax.rem(seq, ratio) * width, width), width)
        mine = lambda c: rbuf.at[lax.div(seq, ratio), c, :, lanes]
    exchange = {}
    for c in range(per_dev):
        rows = jnp.concatenate(
            [abuf[slot_of(partner[m] * per_dev + c)] for m in order], axis=0
        )
        product = jnp.dot(rows, wbuf[...], preferred_element_type=F32).astype(BF16)
        for at, m in enumerate(order):
            block = product[at * STRETCH:(at + 1) * STRETCH]
            if m == 0:
                mine(c)[...] = block
            else:
                psend[m - 1, c] = block
                copy = remote(
                    psend.at[m - 1, c], mine(c), p_send.at[m, c], p_recv.at[seq, c],
                    (seg, partner[m], tp),
                )
                copy.start()
                exchange[m, c] = copy

    last = n_tp - 1

    def arrived(target, c):
        for j in range(ratio):
            origin = target * ratio + j

            @pl.when(origin != seq)
            def _():
                remote(
                    psend.at[0, c], psend.at[0, c], p_send.at[0, c], p_recv.at[origin, c],
                    (seg, partner[1], tp),
                ).wait_recv()

    def along(buf, send, recv, c, d, device):
        return remote(buf.at[d, c], buf.at[d - 1, c], send.at[d, c], recv.at[d - 1, c], device)

    def here(buf, send, recv, c, d, device):
        return remote(buf.at[d, c], buf.at[d, c], send.at[d, c], recv.at[d, c], device)

    def push(buf, send, recv, c, d, target, first, device):
        arrived(target, c)

        @pl.when(first)
        def _():
            buf[d, c] = rbuf[target, c]

        if d < last:

            @pl.when(jnp.logical_not(first))
            def _():
                here(buf, send, recv, c, d, device).wait_recv()
                buf[d, c] = (buf[d, c].astype(F32) + rbuf[target, c].astype(F32)).astype(BF16)

        along(buf, send, recv, c, d, device).start()

    loads[3].wait()
    for c in range(per_dev):
        for d in range(last, 0, -1):
            @pl.when(tp + d <= last)
            def _():
                push(upbuf, up_send, up_recv, c, d, tp + d, tp == 0, (seg, seq, tp + 1))

            @pl.when(tp - d >= 0)
            def _():
                push(downbuf, down_send, down_recv, c, d, tp - d, tp == last, (seg, seq, tp - 1))
        arrived(tp, c)
        for buf, send, recv, end, near in (
            (upbuf, up_send, up_recv, 0, -1),
            (downbuf, down_send, down_recv, last, 1),
        ):
            @pl.when(tp == end)
            def _():
                buf[0, c] = jnp.zeros(buf.shape[2:], buf.dtype)

            @pl.when(tp != end)
            def _():
                here(buf, send, recv, c, 0, (seg, seq, tp + near)).wait_recv()
        own = pl.ds(c * STRETCH, STRETCH)
        total = upbuf[0, c].astype(F32) + downbuf[0, c].astype(F32) + rbuf[tp, c].astype(F32)
        out_ref[own, :] = (resbuf[own, :].astype(F32) + total).astype(out_ref.dtype)

    for copy in pending + list(exchange.values()):
        copy.wait_send()
    for c in range(per_dev):
        for d in range(last, 0, -1):
            @pl.when(tp + d <= last)
            def _():
                along(upbuf, up_send, up_recv, c, d, (seg, seq, tp + 1)).wait_send()

            @pl.when(tp - d >= 0)
            def _():
                along(downbuf, down_send, down_recv, c, d, (seg, seq, tp - 1)).wait_send()


def local(sizes, queries, nb_keys, nb_values, nb_lengths, slot_stretch, out_weight, residual):
    n_seg, n_seq, n_tp = sizes
    per_dev = slot_stretch.shape[1]
    rows, feats = queries.shape[1:]
    span = nb_keys.shape[2]
    width = out_weight.shape[2]
    keep = residual.shape[2]
    table = jnp.pad(slot_stretch, ((0, 7), (0, 128 - per_dev)))
    any_spec = pl.BlockSpec(memory_space=pl.ANY)
    smem_spec = pl.BlockSpec(memory_space=pltpu.SMEM)
    vmem_spec = pl.BlockSpec(memory_space=pltpu.VMEM)
    dma = pltpu.SemaphoreType.DMA
    block = (STRETCH, feats)
    mixed = pl.pallas_call(
        functools.partial(kernel, n_seg, n_seq, n_tp, per_dev),
        out_shape=jax.ShapeDtypeStruct((rows, keep), residual.dtype),
        in_specs=[any_spec] * 5 + [smem_spec] * 2 + [vmem_spec],
        out_specs=vmem_spec,
        scratch_shapes=[
            pltpu.VMEM((per_dev, span, feats), BF16),
            pltpu.VMEM((per_dev, span, feats), BF16),
            pltpu.VMEM((feats, width), BF16),
            pltpu.VMEM((rows, keep), BF16),
            pltpu.VMEM((n_seq * per_dev,) + block, BF16),
            pltpu.VMEM((n_seq * per_dev,) + block, BF16),
            pltpu.VMEM((per_dev,) + block, BF16),
            pltpu.VMEM((n_seq - 1, per_dev, STRETCH, width), BF16),
            pltpu.VMEM((n_tp, per_dev, STRETCH, keep), BF16),
            pltpu.VMEM((n_tp, per_dev, STRETCH, keep), BF16),
            pltpu.VMEM((n_tp, per_dev, STRETCH, keep), BF16),
            pltpu.VMEM((n_seq, 8, 128), jnp.int32),
            pltpu.SMEM((n_seq, 8, 128), jnp.int32),
            dma((5,)),
            dma((per_dev,)), dma((per_dev,)),
            dma((n_seq - 1, per_dev)), dma((n_seq - 1, per_dev)),
            dma((per_dev,)), dma((per_dev,)),
            dma((n_seq - 1, per_dev)), dma((n_seq - 1, per_dev)),
            dma((n_seq,)), dma((n_seq,)),
            dma((n_seq, per_dev)), dma((n_seq, per_dev)),
            dma((n_tp, per_dev)), dma((n_tp, per_dev)),
            dma((n_tp, per_dev)), dma((n_tp, per_dev)),
        ],
        compiler_params=pltpu.CompilerParams(
            collective_id=0, has_side_effects=True, vmem_limit_bytes=48 * 1024 * 1024
        ),
    )(
        queries.reshape(per_dev, STRETCH, feats), nb_keys[0], nb_values[0], out_weight[0],
        residual[0], nb_lengths[0], slot_stretch, table,
    )
    return mixed[None]


def solution(mesh):
    in_specs = (
        P("segment", "seq", "tp"),
        P("segment", "seq", None, "tp"),
        P("segment", "seq", None, "tp"),
        P("segment", "seq", None),
        P("segment", "seq"),
        P("segment", "tp", "seq"),
        P("segment", "seq", "tp"),
    )
    out_specs = P("segment", "seq", "tp")
    sizes = tuple(mesh.shape[name] for name in ("segment", "seq", "tp"))
    return jax.shard_map(
        functools.partial(local, sizes), mesh=mesh, in_specs=in_specs, out_specs=out_specs,
        check_vma=False,
    )
```

```python
import functools
import math

import jax
import jax.numpy as jnp
from jax import lax
from jax.experimental import pallas as pl
from jax.experimental.pallas import tpu as pltpu
from jax.sharding import PartitionSpec as P

HD = 128
STRETCH = 64
NR = 128
GROUPS = 4
MESH = pl.DeviceIdType.MESH
F32 = jnp.float32
BF16 = jnp.bfloat16


def hops(count):
    steps, held = [], [0]
    bit = count // 2
    while bit:
        steps.append((bit, tuple(held)))
        held = held + [mask ^ bit for mask in held]
        bit //= 2
    return steps


def kernel(
    n_seg, n_seq, n_tp, per_dev,
    q_hbm, k_hbm, v_hbm, w_hbm, res_hbm, table_ref,
    out_ref,
    kbuf, vbuf, wbuf, resbuf, qbufs, abufs, answers, acc, psend, rbuf, upbuf, downbuf, tbuf, tsmem, own_smem,
    load_sem, qy_send, qy_recv, qx_send, qx_recv, ay_send, ay_recv, ax_send, ax_recv,
    t_send, t_recv, p_send, p_recv, up_send, up_recv, down_send, down_recv,
):
    seg, seq, tp = lax.axis_index("segment"), lax.axis_index("seq"), lax.axis_index("tp")
    before = lax.rem(seg + n_seg - 1, n_seg)
    after = lax.rem(seg + 1, n_seg)
    span = k_hbm.shape[1]
    feats = q_hbm.shape[2]
    width = w_hbm.shape[1]
    ratio = n_seq // n_tp
    groups = len(qbufs)
    part = feats // groups

    def xor(mask):
        out, bit = seq, 1
        while bit <= mask:
            if mask & bit:
                digit = lax.rem(lax.div(seq, bit), 2)
                out = out + bit - 2 * bit * digit
            bit *= 2
        return out

    partner = [xor(mask) for mask in range(n_seq)]

    loads = [
        pltpu.make_async_copy(src, dst, load_sem.at[i])
        for i, (src, dst) in enumerate(
            [(k_hbm, kbuf), (v_hbm, vbuf), (w_hbm, wbuf), (res_hbm, resbuf), (table_ref, own_smem)]
        )
    ]

    barrier = pltpu.get_barrier_semaphore()

    def greet(device):
        pl.semaphore_signal(barrier, inc=1, device_id=device, device_id_type=MESH)

    sections = [after] if n_seg == 2 else [before, after]
    for mask in range(n_seq):
        for section in sections:
            greet((section, partner[mask], tp))
        if mask:
            greet((seg, partner[mask], tp))

    @pl.when(tp > 0)
    def _():
        greet((seg, seq, tp - 1))

    @pl.when(tp < n_tp - 1)
    def _():
        greet((seg, seq, tp + 1))

    for load in loads:
        load.start()
    line = jnp.int32(2) - (tp == 0).astype(jnp.int32) - (tp == n_tp - 1).astype(jnp.int32)
    pl.semaphore_wait(barrier, len(sections) * n_seq + n_seq - 1 + line)

    def remote(src, dst, send, recv, device):
        return pltpu.make_async_remote_copy(
            src_ref=src, dst_ref=dst, send_sem=send, recv_sem=recv,
            device_id=device, device_id_type=MESH,
        )

    pending = []

    own_rows = pl.ds(seq * per_dev, per_dev)
    qy = [
        remote(
            q_hbm.at[:, :, pl.ds(g * part, part)], qbufs[g].at[own_rows],
            qy_send.at[g], qy_recv.at[g], (before, seq, tp),
        )
        for g in range(groups)
    ]
    for copy in qy:
        copy.start()
    pending += qy

    tables = [
        remote(table_ref, tbuf.at[seq], t_send.at[m], t_recv.at[m], (after, partner[m], tp))
        for m in range(n_seq)
    ]
    for copy in tables:
        copy.start()
    pending += tables

    steps = hops(n_seq)

    def spread(buf, send, recv, g):
        levels, at = [], 0
        for bit, held in steps:
            level = []
            for mask in held:
                place = buf.at[pl.ds(partner[mask] * per_dev, per_dev)]
                level.append(
                    remote(place, place, send.at[at, g], recv.at[at, g], (seg, partner[bit], tp))
                )
                at += 1
            levels.append(level)
        return levels

    def enter(first, levels):
        first.wait_recv()
        for level in levels:
            level[0].start()

    def relay(levels, depth):
        bit, held = steps[depth]
        for mask, copy in zip(held, levels[depth]):
            copy.wait_recv()
            for later in range(depth + 1, len(steps)):
                levels[later][steps[later][1].index(mask ^ bit)].start()

    q_levels = [spread(qbufs[g], qx_send, qx_recv, g) for g in range(groups)]
    a_levels = [spread(abufs[g], ax_send, ax_recv, g) for g in range(groups)]
    ay = [
        remote(answers[g], abufs[g].at[own_rows], ay_send.at[g], ay_recv.at[g], (after, seq, tp))
        for g in range(groups)
    ]
    pending += [copy for levels in q_levels + a_levels for level in levels for copy in level]
    pending += ay

    position = lax.broadcasted_iota(jnp.int32, (1, span), 1)

    def attend(g):
        if g == 0:
            loads[4].wait()
            loads[0].wait()
            loads[1].wait()
        for k in range(per_dev):
            limit = jnp.zeros((1, span), jnp.int32)
            for j in range(span // NR):
                inside = (position >= j * NR) & (position < (j + 1) * NR)
                limit = jnp.where(inside, j * NR + own_smem[1 + k, j], limit)
            valid = position < limit
            stretch = own_smem[0, k]
            for h in range(part // HD):
                cols = pl.ds(h * HD, HD)
                wide = pl.ds(g * part + h * HD, HD)
                query = qbufs[g][stretch, :, cols]
                scores = lax.dot_general(
                    query, kbuf[k, :, wide], (((1,), (1,)), ((), ())), preferred_element_type=F32
                ) * (1.0 / math.sqrt(HD))
                highest = jnp.max(jnp.where(valid, scores, -1e30), axis=1, keepdims=True)
                expo = jnp.exp(jnp.where(valid, scores - highest, -1e30))
                weights = (expo / jnp.sum(expo, axis=1, keepdims=True)).astype(BF16)
                answers[g][k, :, cols] = jnp.dot(
                    weights, vbuf[k, :, wide], preferred_element_type=F32
                ).astype(BF16)
        ay[g].start()

    order = list(range(n_seq - 1, -1, -1))
    if ratio == 1:
        mine = lambda c: rbuf.at[seq, c]
    else:
        lanes = pl.ds(pl.multiple_of(lax.rem(seq, ratio) * width, width), width)
        mine = lambda c: rbuf.at[lax.div(seq, ratio), c, :, lanes]
    exchange = {}
    slots = {}

    def find_slots():
        for copy in tables:
            copy.wait_recv()
        scalars = pltpu.make_async_copy(tbuf, tsmem, load_sem.at[5])
        scalars.start()
        scalars.wait()
        served = [tsmem[g // per_dev, 0, g % per_dev] for g in range(n_seq * per_dev)]
        for m in order:
            for c in range(per_dev):
                slot = jnp.int32(0)
                for g, value in enumerate(served):
                    slot = jnp.where(value == partner[m] * per_dev + c, jnp.int32(g), slot)
                slots[m, c] = slot

    def project(g):
        if g == 0:
            find_slots()
            loads[2].wait()
        for c in range(per_dev):
            rows = jnp.concatenate([abufs[g][slots[m, c]] for m in order], axis=0)
            product = jnp.dot(
                rows, wbuf[pl.ds(g * part, part), :], preferred_element_type=F32
            )
            if g:
                product = acc[c] + product
            if g < groups - 1:
                acc[c] = product
                continue
            product = product.astype(BF16)
            for at, m in enumerate(order):
                block = product[at * STRETCH:(at + 1) * STRETCH]
                if m == 0:
                    mine(c)[...] = block
                else:
                    psend[m - 1, c] = block
                    copy = remote(
                        psend.at[m - 1, c], mine(c), p_send.at[m, c], p_recv.at[seq, c],
                        (seg, partner[m], tp),
                    )
                    copy.start()
                    exchange[m, c] = copy

    depth = len(steps)
    stages = [lambda g: enter(qy[g], q_levels[g])]
    stages += [lambda g, d=d: relay(q_levels[g], d) for d in range(depth)]
    stages[-1] = lambda g: (relay(q_levels[g], depth - 1), attend(g))
    stages += [lambda g: enter(ay[g], a_levels[g])]
    stages += [lambda g, d=d: relay(a_levels[g], d) for d in range(depth)]
    stages[-1] = lambda g: (relay(a_levels[g], depth - 1), project(g))
    delay = [at + (at > depth) for at in range(len(stages))]
    for turn in range(groups + delay[-1]):
        for stage, late in zip(stages, delay):
            if 0 <= turn - late < groups:
                stage(turn - late)

    last = n_tp - 1

    def arrived(target, c):
        for j in range(ratio):
            origin = target * ratio + j

            @pl.when(origin != seq)
            def _():
                remote(
                    psend.at[0, c], psend.at[0, c], p_send.at[0, c], p_recv.at[origin, c],
                    (seg, partner[1], tp),
                ).wait_recv()

    def along(buf, send, recv, c, target, device):
        place = buf.at[target, c]
        return remote(place, place, send.at[target, c], recv.at[target, c], device)

    def push(buf, send, recv, c, target, first, device):
        @pl.when(first)
        def _():
            buf[target, c] = rbuf[target, c]

        @pl.when(jnp.logical_not(first))
        def _():
            along(buf, send, recv, c, target, device).wait_recv()
            buf[target, c] = (buf[target, c].astype(F32) + rbuf[target, c].astype(F32)).astype(BF16)

        along(buf, send, recv, c, target, device).start()

    def finish(c):
        for buf, send, recv, end, near in (
            (upbuf, up_send, up_recv, 0, -1),
            (downbuf, down_send, down_recv, last, 1),
        ):
            @pl.when(tp == end)
            def _():
                buf[tp, c] = jnp.zeros(buf.shape[2:], buf.dtype)

            @pl.when(tp != end)
            def _():
                along(buf, send, recv, c, tp, (seg, seq, tp + near)).wait_recv()
        own = pl.ds(c * STRETCH, STRETCH)
        total = upbuf[tp, c].astype(F32) + downbuf[tp, c].astype(F32) + rbuf[tp, c].astype(F32)
        out_ref[own, :] = (resbuf[own, :].astype(F32) + total).astype(out_ref.dtype)

    home = lax.div(seq, ratio)
    near = n_tp // 2
    visits = [(m, c) for m in range(near) for c in range(per_dev)]
    visits += [(m, c) for c in range(per_dev) for m in range(n_tp - 1, near - 1, -1)]
    targets = {}
    for m in range(n_tp):
        target, bit = home, 1
        while bit <= m:
            if m & bit:
                target = target + bit - 2 * bit * lax.rem(lax.div(home, bit), 2)
            bit *= 2
        targets[m] = target
    loads[3].wait()
    for m, c in visits:
        target = targets[m]
        arrived(target, c)

        @pl.when(target > tp)
        def _():
            push(upbuf, up_send, up_recv, c, target, tp == 0, (seg, seq, tp + 1))

        @pl.when(target < tp)
        def _():
            push(downbuf, down_send, down_recv, c, target, tp == last, (seg, seq, tp - 1))

    for c in range(per_dev):
        finish(c)

    for copy in pending + list(exchange.values()):
        copy.wait_send()
    for m, c in visits:
        target = targets[m]

        @pl.when(target > tp)
        def _():
            along(upbuf, up_send, up_recv, c, target, (seg, seq, tp + 1)).wait_send()

        @pl.when(target < tp)
        def _():
            along(downbuf, down_send, down_recv, c, target, (seg, seq, tp - 1)).wait_send()


def local(sizes, queries, nb_keys, nb_values, nb_lengths, slot_stretch, out_weight, residual):
    n_seg, n_seq, n_tp = sizes
    per_dev = slot_stretch.shape[1]
    rows, feats = queries.shape[1:]
    span = nb_keys.shape[2]
    width = out_weight.shape[2]
    keep = residual.shape[2]
    lengths = nb_lengths[0]
    table = jnp.pad(slot_stretch, ((0, 7), (0, 128 - per_dev)))
    table += jnp.pad(lengths, ((1, 7 - per_dev), (0, 128 - lengths.shape[1])))
    any_spec = pl.BlockSpec(memory_space=pl.ANY)
    vmem_spec = pl.BlockSpec(memory_space=pltpu.VMEM)
    dma = pltpu.SemaphoreType.DMA
    block = (STRETCH, feats // GROUPS)
    mixed = pl.pallas_call(
        functools.partial(kernel, n_seg, n_seq, n_tp, per_dev),
        out_shape=jax.ShapeDtypeStruct((rows, keep), residual.dtype),
        in_specs=[any_spec] * 5 + [vmem_spec],
        out_specs=vmem_spec,
        scratch_shapes=[
            pltpu.VMEM((per_dev, span, feats), BF16),
            pltpu.VMEM((per_dev, span, feats), BF16),
            pltpu.VMEM((feats, width), BF16),
            pltpu.VMEM((rows, keep), BF16),
            [pltpu.VMEM((n_seq * per_dev,) + block, BF16)] * GROUPS,
            [pltpu.VMEM((n_seq * per_dev,) + block, BF16)] * GROUPS,
            [pltpu.VMEM((per_dev,) + block, BF16)] * GROUPS,
            pltpu.VMEM((per_dev, n_seq * STRETCH, width), F32),
            pltpu.VMEM((n_seq - 1, per_dev, STRETCH, width), BF16),
            pltpu.VMEM((n_tp, per_dev, STRETCH, keep), BF16),
            pltpu.VMEM((n_tp, per_dev, STRETCH, keep), BF16),
            pltpu.VMEM((n_tp, per_dev, STRETCH, keep), BF16),
            pltpu.VMEM((n_seq, 8, 128), jnp.int32),
            pltpu.SMEM((n_seq, 8, 128), jnp.int32),
            pltpu.SMEM((8, 128), jnp.int32),
            dma((6,)),
            dma((GROUPS,)), dma((GROUPS,)),
            dma((n_seq - 1, GROUPS)), dma((n_seq - 1, GROUPS)),
            dma((GROUPS,)), dma((GROUPS,)),
            dma((n_seq - 1, GROUPS)), dma((n_seq - 1, GROUPS)),
            dma((n_seq,)), dma((n_seq,)),
            dma((n_seq, per_dev)), dma((n_seq, per_dev)),
            dma((n_tp, per_dev)), dma((n_tp, per_dev)),
            dma((n_tp, per_dev)), dma((n_tp, per_dev)),
        ],
        compiler_params=pltpu.CompilerParams(
            collective_id=0, has_side_effects=True, vmem_limit_bytes=60 * 1024 * 1024
        ),
    )(
        queries.reshape(per_dev, STRETCH, feats), nb_keys[0], nb_values[0], out_weight[0],
        residual[0], table,
    )
    return mixed[None]


def solution(mesh):
    in_specs = (
        P("segment", "seq", "tp"),
        P("segment", "seq", None, "tp"),
        P("segment", "seq", None, "tp"),
        P("segment", "seq", None),
        P("segment", "seq"),
        P("segment", "tp", "seq"),
        P("segment", "seq", "tp"),
    )
    out_specs = P("segment", "seq", "tp")
    sizes = tuple(mesh.shape[name] for name in ("segment", "seq", "tp"))
    return jax.shard_map(
        functools.partial(local, sizes), mesh=mesh, in_specs=in_specs, out_specs=out_specs,
        check_vma=False,
    )
```

```python
import functools
import math

import jax
import jax.numpy as jnp
from jax import lax
from jax.experimental import pallas as pl
from jax.experimental.pallas import tpu as pltpu
from jax.sharding import PartitionSpec as P

HD = 128
STRETCH = 64
NR = 128
GROUPS = 4
MESH = pl.DeviceIdType.MESH
F32 = jnp.float32
BF16 = jnp.bfloat16


def hops(count):
    steps, held = [], [0]
    bit = count // 2
    while bit:
        steps.append((bit, tuple(held)))
        held = held + [mask ^ bit for mask in held]
        bit //= 2
    return steps


def kernel(
    n_seg, n_seq, n_tp, per_dev,
    q_hbm, k_hbm, v_hbm, w_hbm, res_hbm, len_ref, slot_ref, row_ref,
    out_ref,
    kbuf, vbuf, wbuf, resbuf, qbufs, abufs, answers, acc, psend, rbuf, upbuf, downbuf, table, tbuf, tsmem,
    load_sem, qy_send, qy_recv, qx_send, qx_recv, ay_send, ay_recv, ax_send, ax_recv,
    t_send, t_recv, p_send, p_recv, up_send, up_recv, down_send, down_recv,
):
    seg, seq, tp = lax.axis_index("segment"), lax.axis_index("seq"), lax.axis_index("tp")
    before = lax.rem(seg + n_seg - 1, n_seg)
    after = lax.rem(seg + 1, n_seg)
    span = k_hbm.shape[1]
    feats = q_hbm.shape[2]
    width = w_hbm.shape[1]
    ratio = n_seq // n_tp
    groups = len(qbufs)
    part = feats // groups

    def xor(mask):
        out, bit = seq, 1
        while bit <= mask:
            if mask & bit:
                digit = lax.rem(lax.div(seq, bit), 2)
                out = out + bit - 2 * bit * digit
            bit *= 2
        return out

    partner = [xor(mask) for mask in range(n_seq)]

    loads = [
        pltpu.make_async_copy(src, dst, load_sem.at[i])
        for i, (src, dst) in enumerate(
            [(k_hbm, kbuf), (v_hbm, vbuf), (w_hbm, wbuf), (res_hbm, resbuf)]
        )
    ]

    barrier = pltpu.get_barrier_semaphore()

    def greet(device):
        pl.semaphore_signal(barrier, inc=1, device_id=device, device_id_type=MESH)

    sections = [after] if n_seg == 2 else [before, after]
    for mask in range(n_seq):
        for section in sections:
            greet((section, partner[mask], tp))
        if mask:
            greet((seg, partner[mask], tp))

    @pl.when(tp > 0)
    def _():
        greet((seg, seq, tp - 1))

    @pl.when(tp < n_tp - 1)
    def _():
        greet((seg, seq, tp + 1))

    for load in loads:
        load.start()
    table[...] = jnp.zeros(table.shape, table.dtype)
    table[0:1, 0:per_dev] = row_ref[...]
    line = jnp.int32(2) - (tp == 0).astype(jnp.int32) - (tp == n_tp - 1).astype(jnp.int32)
    pl.semaphore_wait(barrier, len(sections) * n_seq + n_seq - 1 + line)

    def remote(src, dst, send, recv, device):
        return pltpu.make_async_remote_copy(
            src_ref=src, dst_ref=dst, send_sem=send, recv_sem=recv,
            device_id=device, device_id_type=MESH,
        )

    pending = []

    own_rows = pl.ds(seq * per_dev, per_dev)
    qy = [
        remote(
            q_hbm.at[:, :, pl.ds(g * part, part)], qbufs[g].at[own_rows],
            qy_send.at[g], qy_recv.at[g], (before, seq, tp),
        )
        for g in range(groups)
    ]
    for copy in qy:
        copy.start()
    pending += qy

    tables = [
        remote(table, tbuf.at[seq], t_send.at[m], t_recv.at[m], (after, partner[m], tp))
        for m in range(n_seq)
    ]
    for copy in tables:
        copy.start()
    pending += tables

    steps = hops(n_seq)

    def spread(buf, send, recv, g):
        levels, at = [], 0
        for bit, held in steps:
            level = []
            for mask in held:
                place = buf.at[pl.ds(partner[mask] * per_dev, per_dev)]
                level.append(
                    remote(place, place, send.at[at, g], recv.at[at, g], (seg, partner[bit], tp))
                )
                at += 1
            levels.append(level)
        return levels

    def enter(first, levels):
        first.wait_recv()
        for level in levels:
            level[0].start()

    def relay(levels, depth):
        bit, held = steps[depth]
        for mask, copy in zip(held, levels[depth]):
            copy.wait_recv()
            for later in range(depth + 1, len(steps)):
                levels[later][steps[later][1].index(mask ^ bit)].start()

    q_levels = [spread(qbufs[g], qx_send, qx_recv, g) for g in range(groups)]
    a_levels = [spread(abufs[g], ax_send, ax_recv, g) for g in range(groups)]
    ay = [
        remote(answers[g], abufs[g].at[own_rows], ay_send.at[g], ay_recv.at[g], (after, seq, tp))
        for g in range(groups)
    ]
    pending += [copy for levels in q_levels + a_levels for level in levels for copy in level]
    pending += ay

    position = lax.broadcasted_iota(jnp.int32, (1, span), 1)

    def attend(g):
        if g == 0:
            loads[0].wait()
            loads[1].wait()
        for k in range(per_dev):
            limit = jnp.zeros((1, span), jnp.int32)
            for j in range(span // NR):
                inside = (position >= j * NR) & (position < (j + 1) * NR)
                limit = jnp.where(inside, j * NR + len_ref[j, k], limit)
            valid = position < limit
            stretch = slot_ref[0, k]
            for h in range(part // HD):
                cols = pl.ds(h * HD, HD)
                wide = pl.ds(g * part + h * HD, HD)
                query = qbufs[g][stretch, :, cols]
                scores = lax.dot_general(
                    query, kbuf[k, :, wide], (((1,), (1,)), ((), ())), preferred_element_type=F32
                ) * (1.0 / math.sqrt(HD))
                scores = jnp.where(valid, scores, -1e30)
                expo = jnp.exp(scores - jnp.max(scores, axis=1, keepdims=True))
                weights = (expo * (1.0 / jnp.sum(expo, axis=1, keepdims=True))).astype(BF16)
                answers[g][k, :, cols] = jnp.dot(
                    weights, vbuf[k, :, wide], preferred_element_type=F32
                ).astype(BF16)
        ay[g].start()

    order = list(range(n_seq - 1, -1, -1))
    if ratio == 1:
        mine = lambda c: rbuf.at[seq, c]
    else:
        lanes = pl.ds(pl.multiple_of(lax.rem(seq, ratio) * width, width), width)
        mine = lambda c: rbuf.at[lax.div(seq, ratio), c, :, lanes]
    exchange = {}
    slots = {}

    def find_slots():
        for copy in tables:
            copy.wait_recv()
        scalars = pltpu.make_async_copy(tbuf, tsmem, load_sem.at[4])
        scalars.start()
        scalars.wait()
        served = [tsmem[g // per_dev, 0, g % per_dev] for g in range(n_seq * per_dev)]
        for m in order:
            for c in range(per_dev):
                slot = jnp.int32(0)
                for g, value in enumerate(served):
                    slot = jnp.where(value == partner[m] * per_dev + c, jnp.int32(g), slot)
                slots[m, c] = slot

    def project(g):
        if g == 0:
            find_slots()
            loads[2].wait()
        for c in range(per_dev):
            rows = jnp.concatenate([abufs[g][slots[m, c]] for m in order], axis=0)
            product = jnp.dot(
                rows, wbuf[pl.ds(g * part, part), :], preferred_element_type=F32
            )
            if g:
                product = acc[c] + product
            if g < groups - 1:
                acc[c] = product
                continue
            product = product.astype(BF16)
            for at, m in enumerate(order):
                block = product[at * STRETCH:(at + 1) * STRETCH]
                if m == 0:
                    mine(c)[...] = block
                else:
                    psend[m - 1, c] = block
                    copy = remote(
                        psend.at[m - 1, c], mine(c), p_send.at[m, c], p_recv.at[seq, c],
                        (seg, partner[m], tp),
                    )
                    copy.start()
                    exchange[m, c] = copy

    depth = len(steps)
    stages = [lambda g: enter(qy[g], q_levels[g])]
    stages += [lambda g, d=d: relay(q_levels[g], d) for d in range(depth)]
    stages[-1] = lambda g: (relay(q_levels[g], depth - 1), attend(g))
    stages += [lambda g: enter(ay[g], a_levels[g])]
    stages += [lambda g, d=d: relay(a_levels[g], d) for d in range(depth)]
    stages[-1] = lambda g: (relay(a_levels[g], depth - 1), project(g))
    delay = [at + (at > depth) for at in range(len(stages))]
    for turn in range(groups + delay[-1]):
        for stage, late in zip(stages, delay):
            if 0 <= turn - late < groups:
                stage(turn - late)

    last = n_tp - 1

    def arrived(target, c):
        for j in range(ratio):
            origin = target * ratio + j

            @pl.when(origin != seq)
            def _():
                remote(
                    psend.at[0, c], psend.at[0, c], p_send.at[0, c], p_recv.at[origin, c],
                    (seg, partner[1], tp),
                ).wait_recv()

    def along(buf, send, recv, c, target, device):
        place = buf.at[target, c]
        return remote(place, place, send.at[target, c], recv.at[target, c], device)

    def push(buf, send, recv, c, target, first, device):
        @pl.when(first)
        def _():
            buf[target, c] = rbuf[target, c]

        @pl.when(jnp.logical_not(first))
        def _():
            along(buf, send, recv, c, target, device).wait_recv()
            buf[target, c] = (buf[target, c].astype(F32) + rbuf[target, c].astype(F32)).astype(BF16)

        along(buf, send, recv, c, target, device).start()

    def finish(c):
        for buf, send, recv, end, near in (
            (upbuf, up_send, up_recv, 0, -1),
            (downbuf, down_send, down_recv, last, 1),
        ):
            @pl.when(tp == end)
            def _():
                buf[tp, c] = jnp.zeros(buf.shape[2:], buf.dtype)

            @pl.when(tp != end)
            def _():
                along(buf, send, recv, c, tp, (seg, seq, tp + near)).wait_recv()
        own = pl.ds(c * STRETCH, STRETCH)
        total = upbuf[tp, c].astype(F32) + downbuf[tp, c].astype(F32) + rbuf[tp, c].astype(F32)
        out_ref[own, :] = (resbuf[own, :].astype(F32) + total).astype(out_ref.dtype)

    home = lax.div(seq, ratio)
    near = n_tp // 2
    low = home < near
    targets = [jnp.where(low, p, last - p) for p in range(near)]
    targets += [jnp.where(low, last - p, p) for p in range(near)]
    visits = [(m, c) for c in range(per_dev) for m in range(near)]
    visits += [(m, c) for c in range(per_dev) for m in range(near, n_tp)]
    loads[3].wait()
    for m, c in visits:
        target = targets[m]
        arrived(target, c)

        @pl.when(target > tp)
        def _():
            push(upbuf, up_send, up_recv, c, target, tp == 0, (seg, seq, tp + 1))

        @pl.when(target < tp)
        def _():
            push(downbuf, down_send, down_recv, c, target, tp == last, (seg, seq, tp - 1))

    for c in range(per_dev):
        finish(c)

    for copy in pending + list(exchange.values()):
        copy.wait_send()
    for m, c in visits:
        target = targets[m]

        @pl.when(target > tp)
        def _():
            along(upbuf, up_send, up_recv, c, target, (seg, seq, tp + 1)).wait_send()

        @pl.when(target < tp)
        def _():
            along(downbuf, down_send, down_recv, c, target, (seg, seq, tp - 1)).wait_send()


def local(sizes, queries, nb_keys, nb_values, nb_lengths, slot_stretch, out_weight, residual):
    n_seg, n_seq, n_tp = sizes
    per_dev = slot_stretch.shape[1]
    rows, feats = queries.shape[1:]
    span = nb_keys.shape[2]
    width = out_weight.shape[2]
    keep = residual.shape[2]
    any_spec = pl.BlockSpec(memory_space=pl.ANY)
    smem_spec = pl.BlockSpec(memory_space=pltpu.SMEM)
    vmem_spec = pl.BlockSpec(memory_space=pltpu.VMEM)
    dma = pltpu.SemaphoreType.DMA
    block = (STRETCH, feats // GROUPS)
    mixed = pl.pallas_call(
        functools.partial(kernel, n_seg, n_seq, n_tp, per_dev),
        out_shape=jax.ShapeDtypeStruct((rows, keep), residual.dtype),
        in_specs=[any_spec] * 5 + [smem_spec] * 2 + [vmem_spec],
        out_specs=vmem_spec,
        scratch_shapes=[
            pltpu.VMEM((per_dev, span, feats), BF16),
            pltpu.VMEM((per_dev, span, feats), BF16),
            pltpu.VMEM((feats, width), BF16),
            pltpu.VMEM((rows, keep), BF16),
            [pltpu.VMEM((n_seq * per_dev,) + block, BF16)] * GROUPS,
            [pltpu.VMEM((n_seq * per_dev,) + block, BF16)] * GROUPS,
            [pltpu.VMEM((per_dev,) + block, BF16)] * GROUPS,
            pltpu.VMEM((per_dev, n_seq * STRETCH, width), F32),
            pltpu.VMEM((n_seq - 1, per_dev, STRETCH, width), BF16),
            pltpu.VMEM((n_tp, per_dev, STRETCH, keep), BF16),
            pltpu.VMEM((n_tp, per_dev, STRETCH, keep), BF16),
            pltpu.VMEM((n_tp, per_dev, STRETCH, keep), BF16),
            pltpu.VMEM((8, 128), jnp.int32),
            pltpu.VMEM((n_seq, 8, 128), jnp.int32),
            pltpu.SMEM((n_seq, 8, 128), jnp.int32),
            dma((5,)),
            dma((GROUPS,)), dma((GROUPS,)),
            dma((n_seq - 1, GROUPS)), dma((n_seq - 1, GROUPS)),
            dma((GROUPS,)), dma((GROUPS,)),
            dma((n_seq - 1, GROUPS)), dma((n_seq - 1, GROUPS)),
            dma((n_seq,)), dma((n_seq,)),
            dma((n_seq, per_dev)), dma((n_seq, per_dev)),
            dma((n_tp, per_dev)), dma((n_tp, per_dev)),
            dma((n_tp, per_dev)), dma((n_tp, per_dev)),
        ],
        compiler_params=pltpu.CompilerParams(
            collective_id=0, has_side_effects=True, vmem_limit_bytes=60 * 1024 * 1024
        ),
    )(
        queries.reshape(per_dev, STRETCH, feats), nb_keys[0], nb_values[0], out_weight[0],
        residual[0], nb_lengths[0].T, slot_stretch, slot_stretch,
    )
    return mixed[None]


def solution(mesh):
    in_specs = (
        P("segment", "seq", "tp"),
        P("segment", "seq", None, "tp"),
        P("segment", "seq", None, "tp"),
        P("segment", "seq", None),
        P("segment", "seq"),
        P("segment", "tp", "seq"),
        P("segment", "seq", "tp"),
    )
    out_specs = P("segment", "seq", "tp")
    sizes = tuple(mesh.shape[name] for name in ("segment", "seq", "tp"))
    return jax.shard_map(
        functools.partial(local, sizes), mesh=mesh, in_specs=in_specs, out_specs=out_specs,
        check_vma=False,
    )
```

```python
import functools
import math

import jax
import jax.numpy as jnp
from jax import lax
from jax.experimental import pallas as pl
from jax.experimental.pallas import tpu as pltpu
from jax.sharding import PartitionSpec as P

HD = 128
STRETCH = 64
NR = 128
GROUPS = 4
ROWS = 32
MESH = pl.DeviceIdType.MESH
F32 = jnp.float32
BF16 = jnp.bfloat16


def hops(count):
    steps, held = [], [0]
    bit = count // 2
    while bit:
        steps.append((bit, tuple(held)))
        held = held + [mask ^ bit for mask in held]
        bit //= 2
    return steps


def kernel(
    n_seg, n_seq, n_tp, per_dev,
    q_hbm, k_hbm, v_hbm, w_hbm, res_hbm, len_ref, slot_ref, row_ref,
    out_ref,
    kbuf, vbuf, wbuf, resbuf, qbufs, abufs, answers, psend, rbuf, upbuf, downbuf, table, tbuf, tsmem,
    load_sem, qy_send, qy_recv, qx_send, qx_recv, ay_send, ay_recv, ax_send, ax_recv,
    t_send, t_recv, p_send, p_recv, up_send, up_recv, down_send, down_recv,
):
    seg, seq, tp = lax.axis_index("segment"), lax.axis_index("seq"), lax.axis_index("tp")
    before = lax.rem(seg + n_seg - 1, n_seg)
    after = lax.rem(seg + 1, n_seg)
    span = k_hbm.shape[1]
    feats = q_hbm.shape[2]
    width = w_hbm.shape[1]
    ratio = n_seq // n_tp
    chunks = per_dev * STRETCH // ROWS
    groups = len(qbufs)
    part = feats // groups

    def xor(mask):
        out, bit = seq, 1
        while bit <= mask:
            if mask & bit:
                digit = lax.rem(lax.div(seq, bit), 2)
                out = out + bit - 2 * bit * digit
            bit *= 2
        return out

    partner = [xor(mask) for mask in range(n_seq)]

    loads = [
        pltpu.make_async_copy(src, dst, load_sem.at[i])
        for i, (src, dst) in enumerate(
            [(k_hbm, kbuf), (v_hbm, vbuf), (w_hbm, wbuf), (res_hbm, resbuf)]
        )
    ]

    barrier = pltpu.get_barrier_semaphore()

    def greet(device):
        pl.semaphore_signal(barrier, inc=1, device_id=device, device_id_type=MESH)

    sections = [after] if n_seg == 2 else [before, after]
    for mask in range(n_seq):
        for section in sections:
            greet((section, partner[mask], tp))
        if mask:
            greet((seg, partner[mask], tp))

    @pl.when(tp > 0)
    def _():
        greet((seg, seq, tp - 1))

    @pl.when(tp < n_tp - 1)
    def _():
        greet((seg, seq, tp + 1))

    for load in loads:
        load.start()
    table[...] = jnp.zeros(table.shape, table.dtype)
    table[0:1, 0:per_dev] = row_ref[...]
    line = jnp.int32(2) - (tp == 0).astype(jnp.int32) - (tp == n_tp - 1).astype(jnp.int32)
    pl.semaphore_wait(barrier, len(sections) * n_seq + n_seq - 1 + line)

    def remote(src, dst, send, recv, device):
        return pltpu.make_async_remote_copy(
            src_ref=src, dst_ref=dst, send_sem=send, recv_sem=recv,
            device_id=device, device_id_type=MESH,
        )

    pending = []

    own_rows = pl.ds(seq * per_dev, per_dev)
    qy = [
        remote(
            q_hbm.at[:, :, pl.ds(g * part, part)], qbufs[g].at[own_rows],
            qy_send.at[g], qy_recv.at[g], (before, seq, tp),
        )
        for g in range(groups)
    ]
    for copy in qy:
        copy.start()
    pending += qy

    tables = [
        remote(table, tbuf.at[seq], t_send.at[m], t_recv.at[m], (after, partner[m], tp))
        for m in range(n_seq)
    ]
    for copy in tables:
        copy.start()
    pending += tables

    steps = hops(n_seq)

    def spread(buf, send, recv, g):
        levels, at = [], 0
        for bit, held in steps:
            level = []
            for mask in held:
                place = buf.at[pl.ds(partner[mask] * per_dev, per_dev)]
                level.append(
                    remote(place, place, send.at[at, g], recv.at[at, g], (seg, partner[bit], tp))
                )
                at += 1
            levels.append(level)
        return levels

    def enter(first, levels):
        first.wait_recv()
        for level in levels:
            level[0].start()

    def relay(levels, depth):
        bit, held = steps[depth]
        for mask, copy in zip(held, levels[depth]):
            copy.wait_recv()
            for later in range(depth + 1, len(steps)):
                levels[later][steps[later][1].index(mask ^ bit)].start()

    q_levels = [spread(qbufs[g], qx_send, qx_recv, g) for g in range(groups)]
    a_levels = [spread(abufs[g], ax_send, ax_recv, g) for g in range(groups)]
    ay = [
        remote(answers[g], abufs[g].at[own_rows], ay_send.at[g], ay_recv.at[g], (after, seq, tp))
        for g in range(groups)
    ]
    pending += [copy for levels in q_levels + a_levels for level in levels for copy in level]
    pending += ay

    position = lax.broadcasted_iota(jnp.int32, (1, span), 1)

    def attend(g):
        if g == 0:
            loads[0].wait()
            loads[1].wait()
        units = [(k, h) for k in range(per_dev) for h in range(part // HD)]
        wide = [pl.ds(g * part + h * HD, HD) for _, h in units]
        valid = []
        for k in range(per_dev):
            limit = jnp.zeros((1, span), jnp.int32)
            for j in range(span // NR):
                inside = (position >= j * NR) & (position < (j + 1) * NR)
                limit = jnp.where(inside, j * NR + len_ref[j, k], limit)
            valid.append(position < limit)
        scores = [
            lax.dot_general(
                qbufs[g][slot_ref[0, k], :, pl.ds(h * HD, HD)], kbuf[k, :, cols],
                (((1,), (1,)), ((), ())), preferred_element_type=F32,
            )
            for (k, h), cols in zip(units, wide)
        ]
        scores = [
            jnp.where(valid[k], one * (1.0 / math.sqrt(HD)), -1e30)
            for (k, _), one in zip(units, scores)
        ]
        highest = [jnp.max(one, axis=1, keepdims=True) for one in scores]
        expo = [jnp.exp(one - top) for one, top in zip(scores, highest)]
        sums = [jnp.sum(one, axis=1, keepdims=True) for one in expo]
        weights = [(one * (1.0 / total)).astype(BF16) for one, total in zip(expo, sums)]
        for (k, h), cols, one in zip(units, wide, weights):
            answers[g][k, :, pl.ds(h * HD, HD)] = jnp.dot(
                one, vbuf[k, :, cols], preferred_element_type=F32
            ).astype(BF16)
        ay[g].start()

    order = list(range(n_seq - 1, -1, -1))
    if ratio == 1:
        mine = lambda c: rbuf.at[seq, c]
    else:
        lanes = pl.ds(pl.multiple_of(lax.rem(seq, ratio) * width, width), width)
        mine = lambda c: rbuf.at[lax.div(seq, ratio), c, :, lanes]
    exchange = {}
    slots = {}

    def find_slots():
        for copy in tables:
            copy.wait_recv()
        scalars = pltpu.make_async_copy(tbuf, tsmem, load_sem.at[4])
        scalars.start()
        scalars.wait()
        served = [tsmem[g // per_dev, 0, g % per_dev] for g in range(n_seq * per_dev)]
        for m in order:
            for c in range(per_dev):
                slot = jnp.int32(0)
                for g, value in enumerate(served):
                    slot = jnp.where(value == partner[m] * per_dev + c, jnp.int32(g), slot)
                slots[m, c] = slot

    def project():
        for k in range(per_dev):
            rows = [
                jnp.concatenate([buf[slots[m, k]] for buf in abufs], axis=1) for m in order
            ]
            product = jnp.dot(
                jnp.concatenate(rows, axis=0), wbuf[...], preferred_element_type=F32
            ).astype(BF16)
            for piece in range(STRETCH // ROWS):
                c = k * (STRETCH // ROWS) + piece
                for at, m in enumerate(order):
                    start = at * STRETCH + piece * ROWS
                    block = product[start:start + ROWS]
                    if m == 0:
                        mine(c)[...] = block
                    else:
                        psend[m - 1, c] = block
                        copy = remote(
                            psend.at[m - 1, c], mine(c), p_send.at[m, c], p_recv.at[seq, c],
                            (seg, partner[m], tp),
                        )
                        copy.start()
                        exchange[m, c] = copy

    depth = len(steps)
    stages = [lambda g: enter(qy[g], q_levels[g])]
    stages += [lambda g, d=d: relay(q_levels[g], d) for d in range(depth)]
    stages[-1] = lambda g: (relay(q_levels[g], depth - 1), attend(g))
    stages += [lambda g: enter(ay[g], a_levels[g])]
    stages += [lambda g, d=d: relay(a_levels[g], d) for d in range(depth)]
    delay = [at + (at > depth) for at in range(len(stages))]
    for turn in range(groups + delay[-1]):
        for stage, late in zip(stages, delay):
            if 0 <= turn - late < groups:
                stage(turn - late)
        if turn == groups:
            find_slots()
    loads[2].wait()
    project()

    last = n_tp - 1

    def arrived(target, c):
        for j in range(ratio):
            origin = target * ratio + j

            @pl.when(origin != seq)
            def _():
                remote(
                    psend.at[0, c], psend.at[0, c], p_send.at[0, c], p_recv.at[origin, c],
                    (seg, partner[1], tp),
                ).wait_recv()

    def along(buf, send, recv, c, target, device):
        place = buf.at[target, c]
        return remote(place, place, send.at[target, c], recv.at[target, c], device)

    def push(buf, send, recv, c, target, first, device):
        @pl.when(first)
        def _():
            buf[target, c] = rbuf[target, c]

        @pl.when(jnp.logical_not(first))
        def _():
            along(buf, send, recv, c, target, device).wait_recv()
            buf[target, c] = (buf[target, c].astype(F32) + rbuf[target, c].astype(F32)).astype(BF16)

        along(buf, send, recv, c, target, device).start()

    def finish(c):
        for buf, send, recv, end, near in (
            (upbuf, up_send, up_recv, 0, -1),
            (downbuf, down_send, down_recv, last, 1),
        ):
            @pl.when(tp == end)
            def _():
                buf[tp, c] = jnp.zeros(buf.shape[2:], buf.dtype)

            @pl.when(tp != end)
            def _():
                along(buf, send, recv, c, tp, (seg, seq, tp + near)).wait_recv()
        own = pl.ds(c * ROWS, ROWS)
        total = upbuf[tp, c].astype(F32) + downbuf[tp, c].astype(F32) + rbuf[tp, c].astype(F32)
        out_ref[own, :] = (resbuf[own, :].astype(F32) + total).astype(out_ref.dtype)

    home = lax.div(seq, ratio)
    near = n_tp // 2
    low = home < near
    targets = [jnp.where(low, p, last - p) for p in range(near)]
    targets += [jnp.where(low, last - p, p) for p in range(near)]
    visits = [(m, c) for c in range(chunks) for m in range(near)]
    visits += [(m, c) for c in range(chunks) for m in range(near, n_tp)]
    loads[3].wait()
    for m, c in visits:
        target = targets[m]
        arrived(target, c)

        @pl.when(target > tp)
        def _():
            push(upbuf, up_send, up_recv, c, target, tp == 0, (seg, seq, tp + 1))

        @pl.when(target < tp)
        def _():
            push(downbuf, down_send, down_recv, c, target, tp == last, (seg, seq, tp - 1))

    for c in range(chunks):
        finish(c)

    for copy in pending + list(exchange.values()):
        copy.wait_send()
    for m, c in visits:
        target = targets[m]

        @pl.when(target > tp)
        def _():
            along(upbuf, up_send, up_recv, c, target, (seg, seq, tp + 1)).wait_send()

        @pl.when(target < tp)
        def _():
            along(downbuf, down_send, down_recv, c, target, (seg, seq, tp - 1)).wait_send()


def local(sizes, queries, nb_keys, nb_values, nb_lengths, slot_stretch, out_weight, residual):
    n_seg, n_seq, n_tp = sizes
    per_dev = slot_stretch.shape[1]
    rows, feats = queries.shape[1:]
    span = nb_keys.shape[2]
    width = out_weight.shape[2]
    keep = residual.shape[2]
    any_spec = pl.BlockSpec(memory_space=pl.ANY)
    smem_spec = pl.BlockSpec(memory_space=pltpu.SMEM)
    vmem_spec = pl.BlockSpec(memory_space=pltpu.VMEM)
    dma = pltpu.SemaphoreType.DMA
    block = (STRETCH, feats // GROUPS)
    chunks = per_dev * STRETCH // ROWS
    mixed = pl.pallas_call(
        functools.partial(kernel, n_seg, n_seq, n_tp, per_dev),
        out_shape=jax.ShapeDtypeStruct((rows, keep), residual.dtype),
        in_specs=[any_spec] * 5 + [smem_spec] * 2 + [vmem_spec],
        out_specs=vmem_spec,
        scratch_shapes=[
            pltpu.VMEM((per_dev, span, feats), BF16),
            pltpu.VMEM((per_dev, span, feats), BF16),
            pltpu.VMEM((feats, width), BF16),
            pltpu.VMEM((rows, keep), BF16),
            [pltpu.VMEM((n_seq * per_dev,) + block, BF16)] * GROUPS,
            [pltpu.VMEM((n_seq * per_dev,) + block, BF16)] * GROUPS,
            [pltpu.VMEM((per_dev,) + block, BF16)] * GROUPS,
            pltpu.VMEM((n_seq - 1, chunks, ROWS, width), BF16),
            pltpu.VMEM((n_tp, chunks, ROWS, keep), BF16),
            pltpu.VMEM((n_tp, chunks, ROWS, keep), BF16),
            pltpu.VMEM((n_tp, chunks, ROWS, keep), BF16),
            pltpu.VMEM((8, 128), jnp.int32),
            pltpu.VMEM((n_seq, 8, 128), jnp.int32),
            pltpu.SMEM((n_seq, 8, 128), jnp.int32),
            dma((5,)),
            dma((GROUPS,)), dma((GROUPS,)),
            dma((n_seq - 1, GROUPS)), dma((n_seq - 1, GROUPS)),
            dma((GROUPS,)), dma((GROUPS,)),
            dma((n_seq - 1, GROUPS)), dma((n_seq - 1, GROUPS)),
            dma((n_seq,)), dma((n_seq,)),
            dma((n_seq, chunks)), dma((n_seq, chunks)),
            dma((n_tp, chunks)), dma((n_tp, chunks)),
            dma((n_tp, chunks)), dma((n_tp, chunks)),
        ],
        compiler_params=pltpu.CompilerParams(
            collective_id=0, has_side_effects=True, vmem_limit_bytes=60 * 1024 * 1024
        ),
    )(
        queries.reshape(per_dev, STRETCH, feats), nb_keys[0], nb_values[0], out_weight[0],
        residual[0], nb_lengths[0].T, slot_stretch, slot_stretch,
    )
    return mixed[None]


def solution(mesh):
    in_specs = (
        P("segment", "seq", "tp"),
        P("segment", "seq", None, "tp"),
        P("segment", "seq", None, "tp"),
        P("segment", "seq", None),
        P("segment", "seq"),
        P("segment", "tp", "seq"),
        P("segment", "seq", "tp"),
    )
    out_specs = P("segment", "seq", "tp")
    sizes = tuple(mesh.shape[name] for name in ("segment", "seq", "tp"))
    return jax.shard_map(
        functools.partial(local, sizes), mesh=mesh, in_specs=in_specs, out_specs=out_specs,
        check_vma=False,
    )
```

```python
import functools
import math

import jax
import jax.numpy as jnp
from jax import lax
from jax.experimental import pallas as pl
from jax.experimental.pallas import tpu as pltpu
from jax.sharding import PartitionSpec as P

HD = 128
STRETCH = 64
NR = 128
GROUPS = 4
ROWS = 32
AHEAD = 2
MESH = pl.DeviceIdType.MESH
F32 = jnp.float32
BF16 = jnp.bfloat16


def hops(count):
    steps, held = [], [0]
    bit = count // 2
    while bit:
        steps.append((bit, tuple(held)))
        held = held + [mask ^ bit for mask in held]
        bit //= 2
    return steps


def kernel(
    n_seg, n_seq, n_tp, per_dev,
    q_hbm, k_hbm, v_hbm, w_hbm, res_hbm, len_ref, slot_ref, row_ref,
    out_ref,
    kbuf, vbuf, wbuf, resbuf, qbufs, abufs, answers, psend, rbuf, upbuf, downbuf, table, tbuf, tsmem,
    load_sem, qy_send, qy_recv, qx_send, qx_recv, ay_send, ay_recv, ax_send, ax_recv,
    t_send, t_recv, p_send, p_recv, up_send, up_recv, down_send, down_recv,
):
    seg, seq, tp = lax.axis_index("segment"), lax.axis_index("seq"), lax.axis_index("tp")
    before = lax.rem(seg + n_seg - 1, n_seg)
    after = lax.rem(seg + 1, n_seg)
    span = k_hbm.shape[1]
    feats = q_hbm.shape[2]
    width = w_hbm.shape[1]
    ratio = n_seq // n_tp
    chunks = per_dev * STRETCH // ROWS
    groups = len(qbufs)
    part = feats // groups

    def xor(mask):
        out, bit = seq, 1
        while bit <= mask:
            if mask & bit:
                digit = lax.rem(lax.div(seq, bit), 2)
                out = out + bit - 2 * bit * digit
            bit *= 2
        return out

    partner = [xor(mask) for mask in range(n_seq)]

    loads = [
        pltpu.make_async_copy(src, dst, load_sem.at[i])
        for i, (src, dst) in enumerate(
            [(k_hbm, kbuf), (v_hbm, vbuf), (w_hbm, wbuf), (res_hbm, resbuf)]
        )
    ]

    barrier = pltpu.get_barrier_semaphore()

    def greet(device):
        pl.semaphore_signal(barrier, inc=1, device_id=device, device_id_type=MESH)

    sections = [after] if n_seg == 2 else [before, after]
    for mask in range(n_seq):
        for section in sections:
            greet((section, partner[mask], tp))
        if mask:
            greet((seg, partner[mask], tp))

    @pl.when(tp > 0)
    def _():
        greet((seg, seq, tp - 1))

    @pl.when(tp < n_tp - 1)
    def _():
        greet((seg, seq, tp + 1))

    for load in loads:
        load.start()
    table[...] = jnp.zeros(table.shape, table.dtype)
    table[0:1, 0:per_dev] = row_ref[...]
    line = jnp.int32(2) - (tp == 0).astype(jnp.int32) - (tp == n_tp - 1).astype(jnp.int32)
    pl.semaphore_wait(barrier, len(sections) * n_seq + n_seq - 1 + line)

    def remote(src, dst, send, recv, device):
        return pltpu.make_async_remote_copy(
            src_ref=src, dst_ref=dst, send_sem=send, recv_sem=recv,
            device_id=device, device_id_type=MESH,
        )

    pending = []

    own_rows = pl.ds(seq * per_dev, per_dev)
    qy = [
        remote(
            q_hbm.at[:, :, pl.ds(g * part, part)], qbufs[g].at[own_rows],
            qy_send.at[g], qy_recv.at[g], (before, seq, tp),
        )
        for g in range(groups)
    ]
    for copy in qy[:AHEAD]:
        copy.start()
    pending += qy

    tables = [
        remote(table, tbuf.at[seq], t_send.at[m], t_recv.at[m], (after, partner[m], tp))
        for m in range(n_seq)
    ]
    for copy in tables:
        copy.start()
    pending += tables

    steps = hops(n_seq)

    def spread(buf, send, recv, g):
        levels, at = [], 0
        for bit, held in steps:
            level = []
            for mask in held:
                place = buf.at[pl.ds(partner[mask] * per_dev, per_dev)]
                level.append(
                    remote(place, place, send.at[at, g], recv.at[at, g], (seg, partner[bit], tp))
                )
                at += 1
            levels.append(level)
        return levels

    def enter(first, levels):
        first.wait_recv()
        for level in levels:
            level[0].start()

    def relay(levels, depth):
        bit, held = steps[depth]
        for mask, copy in zip(held, levels[depth]):
            copy.wait_recv()
            for later in range(depth + 1, len(steps)):
                levels[later][steps[later][1].index(mask ^ bit)].start()

    q_levels = [spread(qbufs[g], qx_send, qx_recv, g) for g in range(groups)]
    a_levels = [spread(abufs[g], ax_send, ax_recv, g) for g in range(groups)]
    ay = [
        remote(answers[g], abufs[g].at[own_rows], ay_send.at[g], ay_recv.at[g], (after, seq, tp))
        for g in range(groups)
    ]
    pending += [copy for levels in q_levels + a_levels for level in levels for copy in level]
    pending += ay

    position = lax.broadcasted_iota(jnp.int32, (1, span), 1)

    def attend(g):
        if g == 0:
            loads[0].wait()
            loads[1].wait()
        units = [(k, h) for k in range(per_dev) for h in range(part // HD)]
        wide = [pl.ds(g * part + h * HD, HD) for _, h in units]
        valid = []
        for k in range(per_dev):
            limit = jnp.zeros((1, span), jnp.int32)
            for j in range(span // NR):
                inside = (position >= j * NR) & (position < (j + 1) * NR)
                limit = jnp.where(inside, j * NR + len_ref[j, k], limit)
            valid.append(position < limit)
        scores = [
            lax.dot_general(
                qbufs[g][slot_ref[0, k], :, pl.ds(h * HD, HD)], kbuf[k, :, cols],
                (((1,), (1,)), ((), ())), preferred_element_type=F32,
            )
            for (k, h), cols in zip(units, wide)
        ]
        scores = [
            jnp.where(valid[k], one * (1.0 / math.sqrt(HD)), -1e30)
            for (k, _), one in zip(units, scores)
        ]
        highest = [jnp.max(one, axis=1, keepdims=True) for one in scores]
        expo = [jnp.exp(one - top) for one, top in zip(scores, highest)]
        sums = [jnp.sum(one, axis=1, keepdims=True) for one in expo]
        weights = [(one * (1.0 / total)).astype(BF16) for one, total in zip(expo, sums)]
        for (k, h), cols, one in zip(units, wide, weights):
            answers[g][k, :, pl.ds(h * HD, HD)] = jnp.dot(
                one, vbuf[k, :, cols], preferred_element_type=F32
            ).astype(BF16)
        ay[g].start()

    order = list(range(n_seq - 1, -1, -1))
    if ratio == 1:
        mine = lambda c: rbuf.at[seq, c]
    else:
        lanes = pl.ds(pl.multiple_of(lax.rem(seq, ratio) * width, width), width)
        mine = lambda c: rbuf.at[lax.div(seq, ratio), c, :, lanes]
    exchange = {}
    slots = {}

    def find_slots():
        for copy in tables:
            copy.wait_recv()
        scalars = pltpu.make_async_copy(tbuf, tsmem, load_sem.at[4])
        scalars.start()
        scalars.wait()
        served = [tsmem[g // per_dev, 0, g % per_dev] for g in range(n_seq * per_dev)]
        for m in order:
            for c in range(per_dev):
                slot = jnp.int32(0)
                for g, value in enumerate(served):
                    slot = jnp.where(value == partner[m] * per_dev + c, jnp.int32(g), slot)
                slots[m, c] = slot

    def send_out(c):
        for m in range(1, n_seq):
            exchange[m, c].start()

    def project():
        for k in range(per_dev):
            rows = [
                jnp.concatenate([buf[slots[m, k]] for buf in abufs], axis=1) for m in order
            ]
            product = jnp.dot(
                jnp.concatenate(rows, axis=0), wbuf[...], preferred_element_type=F32
            ).astype(BF16)
            for piece in range(STRETCH // ROWS):
                c = k * (STRETCH // ROWS) + piece
                for at, m in enumerate(order):
                    start = at * STRETCH + piece * ROWS
                    block = product[start:start + ROWS]
                    if m == 0:
                        mine(c)[...] = block
                    else:
                        psend[m - 1, c] = block
                        copy = remote(
                            psend.at[m - 1, c], mine(c), p_send.at[m, c], p_recv.at[seq, c],
                            (seg, partner[m], tp),
                        )
                        exchange[m, c] = copy
                if c < AHEAD:
                    send_out(c)

    depth = len(steps)
    def enter_queries(g):
        enter(qy[g], q_levels[g])
        if g + AHEAD < groups:
            qy[g + AHEAD].start()

    stages = [enter_queries]
    stages += [lambda g, d=d: relay(q_levels[g], d) for d in range(depth)]
    stages[-1] = lambda g: (relay(q_levels[g], depth - 1), attend(g))
    stages += [lambda g: enter(ay[g], a_levels[g])]
    stages += [lambda g, d=d: relay(a_levels[g], d) for d in range(depth)]
    delay = [at + (at > depth) for at in range(len(stages))]
    for turn in range(groups + delay[-1]):
        for stage, late in zip(stages, delay):
            if 0 <= turn - late < groups:
                stage(turn - late)
        if turn == groups:
            find_slots()
    loads[2].wait()
    project()

    last = n_tp - 1

    def arrived(target, c):
        for j in range(ratio):
            origin = target * ratio + j

            @pl.when(origin != seq)
            def _():
                remote(
                    psend.at[0, c], psend.at[0, c], p_send.at[0, c], p_recv.at[origin, c],
                    (seg, partner[1], tp),
                ).wait_recv()

    def along(buf, send, recv, c, target, device):
        place = buf.at[target, c]
        return remote(place, place, send.at[target, c], recv.at[target, c], device)

    def push(buf, send, recv, c, target, first, device):
        @pl.when(first)
        def _():
            buf[target, c] = rbuf[target, c]

        @pl.when(jnp.logical_not(first))
        def _():
            along(buf, send, recv, c, target, device).wait_recv()
            buf[target, c] = (buf[target, c].astype(F32) + rbuf[target, c].astype(F32)).astype(BF16)

        along(buf, send, recv, c, target, device).start()

    def finish(c):
        for buf, send, recv, end, near in (
            (upbuf, up_send, up_recv, 0, -1),
            (downbuf, down_send, down_recv, last, 1),
        ):
            @pl.when(tp == end)
            def _():
                buf[tp, c] = jnp.zeros(buf.shape[2:], buf.dtype)

            @pl.when(tp != end)
            def _():
                along(buf, send, recv, c, tp, (seg, seq, tp + near)).wait_recv()
        own = pl.ds(c * ROWS, ROWS)
        total = upbuf[tp, c].astype(F32) + downbuf[tp, c].astype(F32) + rbuf[tp, c].astype(F32)
        out_ref[own, :] = (resbuf[own, :].astype(F32) + total).astype(out_ref.dtype)

    home = lax.div(seq, ratio)
    near = n_tp // 2
    low = home < near
    targets = [jnp.where(low, p, last - p) for p in range(near)]
    targets += [jnp.where(low, last - p, p) for p in range(near)]
    visits = []
    for step in range(chunks + 1):
        for at in range(near):
            visits += [(m, c) for m, c in ((at, step), (near + at, step - 1)) if 0 <= c < chunks]
    loads[3].wait()
    for m, c in visits:
        target = targets[m]
        if m == 0 and c + AHEAD < chunks:
            send_out(c + AHEAD)
        arrived(target, c)

        @pl.when(target > tp)
        def _():
            push(upbuf, up_send, up_recv, c, target, tp == 0, (seg, seq, tp + 1))

        @pl.when(target < tp)
        def _():
            push(downbuf, down_send, down_recv, c, target, tp == last, (seg, seq, tp - 1))

    for c in range(chunks):
        finish(c)

    for copy in pending + list(exchange.values()):
        copy.wait_send()
    for m, c in visits:
        target = targets[m]

        @pl.when(target > tp)
        def _():
            along(upbuf, up_send, up_recv, c, target, (seg, seq, tp + 1)).wait_send()

        @pl.when(target < tp)
        def _():
            along(downbuf, down_send, down_recv, c, target, (seg, seq, tp - 1)).wait_send()


def local(sizes, queries, nb_keys, nb_values, nb_lengths, slot_stretch, out_weight, residual):
    n_seg, n_seq, n_tp = sizes
    per_dev = slot_stretch.shape[1]
    rows, feats = queries.shape[1:]
    span = nb_keys.shape[2]
    width = out_weight.shape[2]
    keep = residual.shape[2]
    any_spec = pl.BlockSpec(memory_space=pl.ANY)
    smem_spec = pl.BlockSpec(memory_space=pltpu.SMEM)
    vmem_spec = pl.BlockSpec(memory_space=pltpu.VMEM)
    dma = pltpu.SemaphoreType.DMA
    block = (STRETCH, feats // GROUPS)
    chunks = per_dev * STRETCH // ROWS
    mixed = pl.pallas_call(
        functools.partial(kernel, n_seg, n_seq, n_tp, per_dev),
        out_shape=jax.ShapeDtypeStruct((rows, keep), residual.dtype),
        in_specs=[any_spec] * 5 + [smem_spec] * 2 + [vmem_spec],
        out_specs=vmem_spec,
        scratch_shapes=[
            pltpu.VMEM((per_dev, span, feats), BF16),
            pltpu.VMEM((per_dev, span, feats), BF16),
            pltpu.VMEM((feats, width), BF16),
            pltpu.VMEM((rows, keep), BF16),
            [pltpu.VMEM((n_seq * per_dev,) + block, BF16)] * GROUPS,
            [pltpu.VMEM((n_seq * per_dev,) + block, BF16)] * GROUPS,
            [pltpu.VMEM((per_dev,) + block, BF16)] * GROUPS,
            pltpu.VMEM((n_seq - 1, chunks, ROWS, width), BF16),
            pltpu.VMEM((n_tp, chunks, ROWS, keep), BF16),
            pltpu.VMEM((n_tp, chunks, ROWS, keep), BF16),
            pltpu.VMEM((n_tp, chunks, ROWS, keep), BF16),
            pltpu.VMEM((8, 128), jnp.int32),
            pltpu.VMEM((n_seq, 8, 128), jnp.int32),
            pltpu.SMEM((n_seq, 8, 128), jnp.int32),
            dma((5,)),
            dma((GROUPS,)), dma((GROUPS,)),
            dma((n_seq - 1, GROUPS)), dma((n_seq - 1, GROUPS)),
            dma((GROUPS,)), dma((GROUPS,)),
            dma((n_seq - 1, GROUPS)), dma((n_seq - 1, GROUPS)),
            dma((n_seq,)), dma((n_seq,)),
            dma((n_seq, chunks)), dma((n_seq, chunks)),
            dma((n_tp, chunks)), dma((n_tp, chunks)),
            dma((n_tp, chunks)), dma((n_tp, chunks)),
        ],
        compiler_params=pltpu.CompilerParams(
            collective_id=0, has_side_effects=True, vmem_limit_bytes=60 * 1024 * 1024
        ),
    )(
        queries.reshape(per_dev, STRETCH, feats), nb_keys[0], nb_values[0], out_weight[0],
        residual[0], nb_lengths[0].T, slot_stretch, slot_stretch,
    )
    return mixed[None]


def solution(mesh):
    in_specs = (
        P("segment", "seq", "tp"),
        P("segment", "seq", None, "tp"),
        P("segment", "seq", None, "tp"),
        P("segment", "seq", None),
        P("segment", "seq"),
        P("segment", "tp", "seq"),
        P("segment", "seq", "tp"),
    )
    out_specs = P("segment", "seq", "tp")
    sizes = tuple(mesh.shape[name] for name in ("segment", "seq", "tp"))
    return jax.shard_map(
        functools.partial(local, sizes), mesh=mesh, in_specs=in_specs, out_specs=out_specs,
        check_vma=False,
    )
```

```python
import functools
import math

import jax
import jax.numpy as jnp
from jax import lax
from jax.experimental import pallas as pl
from jax.experimental.pallas import tpu as pltpu
from jax.sharding import PartitionSpec as P

HD = 128
STRETCH = 64
NR = 128
GROUPS = 4
ROWS = 32
MESH = pl.DeviceIdType.MESH
F32 = jnp.float32
BF16 = jnp.bfloat16


def hops(count):
    steps, held = [], [0]
    bit = count // 2
    while bit:
        steps.append((bit, tuple(held)))
        held = held + [mask ^ bit for mask in held]
        bit //= 2
    return steps


def kernel(
    n_seg, n_seq, n_tp, per_dev,
    q_hbm, k_hbm, v_hbm, w_hbm, res_hbm, len_ref, slot_ref, row_ref,
    out_ref,
    kbuf, vbuf, wbuf, resbuf, qbufs, abufs, answers, psend, rbuf, upbuf, downbuf, table, tbuf, tsmem,
    load_sem, qy_send, qy_recv, qx_send, qx_recv, ay_send, ay_recv, ax_send, ax_recv,
    t_send, t_recv, p_send, p_recv, up_send, up_recv, down_send, down_recv,
):
    seg, seq, tp = lax.axis_index("segment"), lax.axis_index("seq"), lax.axis_index("tp")
    before = lax.rem(seg + n_seg - 1, n_seg)
    after = lax.rem(seg + 1, n_seg)
    span = k_hbm.shape[1]
    feats = q_hbm.shape[2]
    width = w_hbm.shape[1]
    ratio = n_seq // n_tp
    chunks = per_dev * STRETCH // ROWS
    groups = len(qbufs)
    part = feats // groups

    def xor(mask):
        out, bit = seq, 1
        while bit <= mask:
            if mask & bit:
                digit = lax.rem(lax.div(seq, bit), 2)
                out = out + bit - 2 * bit * digit
            bit *= 2
        return out

    partner = [xor(mask) for mask in range(n_seq)]

    loads = [
        pltpu.make_async_copy(src, dst, load_sem.at[i])
        for i, (src, dst) in enumerate(
            [(k_hbm, kbuf), (v_hbm, vbuf), (w_hbm, wbuf), (res_hbm, resbuf)]
        )
    ]

    barrier = pltpu.get_barrier_semaphore()

    def greet(device):
        pl.semaphore_signal(barrier, inc=1, device_id=device, device_id_type=MESH)

    sections = [after] if n_seg == 2 else [before, after]
    for mask in range(n_seq):
        for section in sections:
            greet((section, partner[mask], tp))
        if mask:
            greet((seg, partner[mask], tp))

    @pl.when(tp > 0)
    def _():
        greet((seg, seq, tp - 1))

    @pl.when(tp < n_tp - 1)
    def _():
        greet((seg, seq, tp + 1))

    for load in loads:
        load.start()
    table[...] = jnp.zeros(table.shape, table.dtype)
    table[0:1, 0:per_dev] = row_ref[...]
    line = jnp.int32(2) - (tp == 0).astype(jnp.int32) - (tp == n_tp - 1).astype(jnp.int32)
    pl.semaphore_wait(barrier, len(sections) * n_seq + n_seq - 1 + line)

    def remote(src, dst, send, recv, device):
        return pltpu.make_async_remote_copy(
            src_ref=src, dst_ref=dst, send_sem=send, recv_sem=recv,
            device_id=device, device_id_type=MESH,
        )

    pending = []

    own_rows = pl.ds(seq * per_dev, per_dev)
    qy = [
        remote(
            q_hbm.at[:, :, pl.ds(g * part, part)], qbufs[g].at[own_rows],
            qy_send.at[g], qy_recv.at[g], (before, seq, tp),
        )
        for g in range(groups)
    ]
    for copy in qy:
        copy.start()
    pending += qy

    tables = [
        remote(table, tbuf.at[seq], t_send.at[m], t_recv.at[m], (after, partner[m], tp))
        for m in range(n_seq)
    ]
    for copy in tables:
        copy.start()
    pending += tables

    steps = hops(n_seq)

    def spread(buf, send, recv, g):
        levels, at = [], 0
        for bit, held in steps:
            level = []
            for mask in held:
                place = buf.at[pl.ds(partner[mask] * per_dev, per_dev)]
                level.append(
                    remote(place, place, send.at[at, g], recv.at[at, g], (seg, partner[bit], tp))
                )
                at += 1
            levels.append(level)
        return levels

    def enter(first, levels):
        first.wait_recv()
        for level in levels:
            level[0].start()

    def relay(levels, depth):
        bit, held = steps[depth]
        for mask, copy in zip(held, levels[depth]):
            copy.wait_recv()
            for later in range(depth + 1, len(steps)):
                levels[later][steps[later][1].index(mask ^ bit)].start()

    q_levels = [spread(qbufs[g], qx_send, qx_recv, g) for g in range(groups)]
    a_levels = [spread(abufs[g], ax_send, ax_recv, g) for g in range(groups)]
    ay = [
        remote(answers[g], abufs[g].at[own_rows], ay_send.at[g], ay_recv.at[g], (after, seq, tp))
        for g in range(groups)
    ]
    pending += [copy for levels in q_levels + a_levels for level in levels for copy in level]
    pending += ay

    position = lax.broadcasted_iota(jnp.int32, (1, span), 1)

    def attend(g):
        if g == 0:
            loads[0].wait()
            loads[1].wait()
        units = [(k, h) for k in range(per_dev) for h in range(part // HD)]
        wide = [pl.ds(g * part + h * HD, HD) for _, h in units]
        valid = []
        for k in range(per_dev):
            limit = jnp.zeros((1, span), jnp.int32)
            for j in range(span // NR):
                inside = (position >= j * NR) & (position < (j + 1) * NR)
                limit = jnp.where(inside, j * NR + len_ref[j, k], limit)
            valid.append(position < limit)
        scores = [
            lax.dot_general(
                qbufs[g][slot_ref[0, k], :, pl.ds(h * HD, HD)], kbuf[k, :, cols],
                (((1,), (1,)), ((), ())), preferred_element_type=F32,
            )
            for (k, h), cols in zip(units, wide)
        ]
        scores = [
            jnp.where(valid[k], one * (1.0 / math.sqrt(HD)), -1e30)
            for (k, _), one in zip(units, scores)
        ]
        highest = [jnp.max(one, axis=1, keepdims=True) for one in scores]
        expo = [jnp.exp(one - top) for one, top in zip(scores, highest)]
        sums = [jnp.sum(one, axis=1, keepdims=True) for one in expo]
        weights = [(one * (1.0 / total)).astype(BF16) for one, total in zip(expo, sums)]
        for (k, h), cols, one in zip(units, wide, weights):
            answers[g][k, :, pl.ds(h * HD, HD)] = jnp.dot(
                one, vbuf[k, :, cols], preferred_element_type=F32
            ).astype(BF16)
        ay[g].start()

    order = list(range(n_seq - 1, -1, -1))
    if ratio == 1:
        mine = lambda c: rbuf.at[seq, c]
    else:
        lanes = pl.ds(pl.multiple_of(lax.rem(seq, ratio) * width, width), width)
        mine = lambda c: rbuf.at[lax.div(seq, ratio), c, :, lanes]
    exchange = {}
    slots = {}

    def find_slots():
        for copy in tables:
            copy.wait_recv()
        scalars = pltpu.make_async_copy(tbuf, tsmem, load_sem.at[4])
        scalars.start()
        scalars.wait()
        served = [tsmem[g // per_dev, 0, g % per_dev] for g in range(n_seq * per_dev)]
        for m in order:
            for c in range(per_dev):
                slot = jnp.int32(0)
                for g, value in enumerate(served):
                    slot = jnp.where(value == partner[m] * per_dev + c, jnp.int32(g), slot)
                slots[m, c] = slot

    def project():
        for k in range(per_dev):
            rows = [
                jnp.concatenate([buf[slots[m, k]] for buf in abufs], axis=1) for m in order
            ]
            product = jnp.dot(
                jnp.concatenate(rows, axis=0), wbuf[...], preferred_element_type=F32
            ).astype(BF16)
            for piece in range(STRETCH // ROWS):
                c = k * (STRETCH // ROWS) + piece
                for at, m in enumerate(order):
                    start = at * STRETCH + piece * ROWS
                    block = product[start:start + ROWS]
                    if m == 0:
                        mine(c)[...] = block
                    else:
                        psend[m - 1, c] = block
                        copy = remote(
                            psend.at[m - 1, c], mine(c), p_send.at[m, c], p_recv.at[seq, c],
                            (seg, partner[m], tp),
                        )
                        copy.start()
                        exchange[m, c] = copy

    depth = len(steps)
    stages = [lambda g: enter(qy[g], q_levels[g])]
    stages += [lambda g, d=d: relay(q_levels[g], d) for d in range(depth)]
    stages[-1] = lambda g: (relay(q_levels[g], depth - 1), attend(g))
    stages += [lambda g: enter(ay[g], a_levels[g])]
    stages += [lambda g, d=d: relay(a_levels[g], d) for d in range(depth)]
    delay = [at + (at > depth) for at in range(len(stages))]
    for turn in range(groups + delay[-1]):
        for stage, late in zip(stages, delay):
            if 0 <= turn - late < groups:
                stage(turn - late)
        if turn == groups:
            find_slots()
    loads[2].wait()
    project()

    last = n_tp - 1

    def arrived(target, c):
        for j in range(ratio):
            origin = target * ratio + j

            @pl.when(origin != seq)
            def _():
                remote(
                    psend.at[0, c], psend.at[0, c], p_send.at[0, c], p_recv.at[origin, c],
                    (seg, partner[1], tp),
                ).wait_recv()

    def along(buf, send, recv, c, target, device):
        place = buf.at[target, c]
        return remote(place, place, send.at[target, c], recv.at[target, c], device)

    def push(buf, send, recv, c, target, first, device):
        @pl.when(first)
        def _():
            buf[target, c] = rbuf[target, c]

        @pl.when(jnp.logical_not(first))
        def _():
            along(buf, send, recv, c, target, device).wait_recv()
            buf[target, c] = (buf[target, c].astype(F32) + rbuf[target, c].astype(F32)).astype(BF16)

        along(buf, send, recv, c, target, device).start()

    def finish(c):
        for buf, send, recv, end, near in (
            (upbuf, up_send, up_recv, 0, -1),
            (downbuf, down_send, down_recv, last, 1),
        ):
            @pl.when(tp == end)
            def _():
                buf[tp, c] = jnp.zeros(buf.shape[2:], buf.dtype)

            @pl.when(tp != end)
            def _():
                along(buf, send, recv, c, tp, (seg, seq, tp + near)).wait_recv()
        own = pl.ds(c * ROWS, ROWS)
        total = upbuf[tp, c].astype(F32) + downbuf[tp, c].astype(F32) + rbuf[tp, c].astype(F32)
        out_ref[own, :] = (resbuf[own, :].astype(F32) + total).astype(out_ref.dtype)

    home = lax.div(seq, ratio)
    near = n_tp // 2
    low = home < near
    targets = [jnp.where(low, p, last - p) for p in range(near)]
    targets += [jnp.where(low, last - p, p) for p in range(near)]
    loads[3].wait()

    def each(step, rise, fall):
        for m, target in enumerate(targets):
            begin = step - m // near
            up, down = begin - tp, begin - (last - tp)

            @pl.when((target > tp) & (up >= 0) & (up < chunks))
            def _():
                rise(target, up)

            @pl.when((target < tp) & (down >= 0) & (down < chunks))
            def _():
                fall(target, down)

    def rise(target, c):
        arrived(target, c)
        push(upbuf, up_send, up_recv, c, target, tp == 0, (seg, seq, tp + 1))

    def fall(target, c):
        arrived(target, c)
        push(downbuf, down_send, down_recv, c, target, tp == last, (seg, seq, tp - 1))

    @pl.loop(0, chunks + 1 + last)
    def _(step):
        each(step, rise, fall)

    for c in range(chunks):
        arrived(tp, c)
        finish(c)

    for copy in pending + list(exchange.values()):
        copy.wait_send()
    @pl.loop(0, chunks + 1 + last)
    def _(step):
        each(
            step,
            lambda target, c: along(
                upbuf, up_send, up_recv, c, target, (seg, seq, tp + 1)
            ).wait_send(),
            lambda target, c: along(
                downbuf, down_send, down_recv, c, target, (seg, seq, tp - 1)
            ).wait_send(),
        )


def local(sizes, queries, nb_keys, nb_values, nb_lengths, slot_stretch, out_weight, residual):
    n_seg, n_seq, n_tp = sizes
    per_dev = slot_stretch.shape[1]
    rows, feats = queries.shape[1:]
    span = nb_keys.shape[2]
    width = out_weight.shape[2]
    keep = residual.shape[2]
    any_spec = pl.BlockSpec(memory_space=pl.ANY)
    smem_spec = pl.BlockSpec(memory_space=pltpu.SMEM)
    vmem_spec = pl.BlockSpec(memory_space=pltpu.VMEM)
    dma = pltpu.SemaphoreType.DMA
    block = (STRETCH, feats // GROUPS)
    chunks = per_dev * STRETCH // ROWS
    mixed = pl.pallas_call(
        functools.partial(kernel, n_seg, n_seq, n_tp, per_dev),
        out_shape=jax.ShapeDtypeStruct((rows, keep), residual.dtype),
        in_specs=[any_spec] * 5 + [smem_spec] * 2 + [vmem_spec],
        out_specs=vmem_spec,
        scratch_shapes=[
            pltpu.VMEM((per_dev, span, feats), BF16),
            pltpu.VMEM((per_dev, span, feats), BF16),
            pltpu.VMEM((feats, width), BF16),
            pltpu.VMEM((rows, keep), BF16),
            [pltpu.VMEM((n_seq * per_dev,) + block, BF16)] * GROUPS,
            [pltpu.VMEM((n_seq * per_dev,) + block, BF16)] * GROUPS,
            [pltpu.VMEM((per_dev,) + block, BF16)] * GROUPS,
            pltpu.VMEM((n_seq - 1, chunks, ROWS, width), BF16),
            pltpu.VMEM((n_tp, chunks, ROWS, keep), BF16),
            pltpu.VMEM((n_tp, chunks, ROWS, keep), BF16),
            pltpu.VMEM((n_tp, chunks, ROWS, keep), BF16),
            pltpu.VMEM((8, 128), jnp.int32),
            pltpu.VMEM((n_seq, 8, 128), jnp.int32),
            pltpu.SMEM((n_seq, 8, 128), jnp.int32),
            dma((5,)),
            dma((GROUPS,)), dma((GROUPS,)),
            dma((n_seq - 1, GROUPS)), dma((n_seq - 1, GROUPS)),
            dma((GROUPS,)), dma((GROUPS,)),
            dma((n_seq - 1, GROUPS)), dma((n_seq - 1, GROUPS)),
            dma((n_seq,)), dma((n_seq,)),
            dma((n_seq, chunks)), dma((n_seq, chunks)),
            dma((n_tp, chunks)), dma((n_tp, chunks)),
            dma((n_tp, chunks)), dma((n_tp, chunks)),
        ],
        compiler_params=pltpu.CompilerParams(
            collective_id=0, has_side_effects=True, vmem_limit_bytes=60 * 1024 * 1024
        ),
    )(
        queries.reshape(per_dev, STRETCH, feats), nb_keys[0], nb_values[0], out_weight[0],
        residual[0], nb_lengths[0].T, slot_stretch, slot_stretch,
    )
    return mixed[None]


def solution(mesh):
    in_specs = (
        P("segment", "seq", "tp"),
        P("segment", "seq", None, "tp"),
        P("segment", "seq", None, "tp"),
        P("segment", "seq", None),
        P("segment", "seq"),
        P("segment", "tp", "seq"),
        P("segment", "seq", "tp"),
    )
    out_specs = P("segment", "seq", "tp")
    sizes = tuple(mesh.shape[name] for name in ("segment", "seq", "tp"))
    return jax.shard_map(
        functools.partial(local, sizes), mesh=mesh, in_specs=in_specs, out_specs=out_specs,
        check_vma=False,
    )
```

```python
import functools
import math

import jax
import jax.numpy as jnp
from jax import lax
from jax.experimental import pallas as pl
from jax.experimental.pallas import tpu as pltpu
from jax.sharding import PartitionSpec as P

HD = 128
STRETCH = 64
NR = 128
GROUPS = 4
ROWS = 32
AHEAD = 2
MESH = pl.DeviceIdType.MESH
F32 = jnp.float32
BF16 = jnp.bfloat16


def hops(count):
    steps, held = [], [0]
    bit = count // 2
    while bit:
        steps.append((bit, tuple(held)))
        held = held + [mask ^ bit for mask in held]
        bit //= 2
    return steps


def kernel(
    n_seg, n_seq, n_tp, per_dev,
    q_hbm, k_hbm, v_hbm, w_hbm, res_hbm, len_ref, slot_ref, row_ref,
    out_ref,
    kbuf, vbuf, wbuf, resbuf, qbufs, abufs, answers, psend, rbuf, upbuf, downbuf, table, tbuf, tsmem,
    load_sem, qy_send, qy_recv, qx_send, qx_recv, ay_send, ay_recv, ax_send, ax_recv,
    t_send, t_recv, p_send, p_recv, up_send, up_recv, down_send, down_recv,
):
    seg, seq, tp = lax.axis_index("segment"), lax.axis_index("seq"), lax.axis_index("tp")
    before = lax.rem(seg + n_seg - 1, n_seg)
    after = lax.rem(seg + 1, n_seg)
    span = k_hbm.shape[1]
    feats = q_hbm.shape[2]
    width = w_hbm.shape[1]
    ratio = n_seq // n_tp
    chunks = per_dev * STRETCH // ROWS
    groups = len(qbufs)
    part = feats // groups

    def xor(mask):
        out, bit = seq, 1
        while bit <= mask:
            if mask & bit:
                digit = lax.rem(lax.div(seq, bit), 2)
                out = out + bit - 2 * bit * digit
            bit *= 2
        return out

    partner = [xor(mask) for mask in range(n_seq)]

    loads = [
        pltpu.make_async_copy(src, dst, load_sem.at[i])
        for i, (src, dst) in enumerate(
            [(k_hbm, kbuf), (v_hbm, vbuf), (w_hbm, wbuf), (res_hbm, resbuf)]
        )
    ]

    barrier = pltpu.get_barrier_semaphore()

    def greet(device):
        pl.semaphore_signal(barrier, inc=1, device_id=device, device_id_type=MESH)

    sections = [after] if n_seg == 2 else [before, after]
    for mask in range(n_seq):
        for section in sections:
            greet((section, partner[mask], tp))
        if mask:
            greet((seg, partner[mask], tp))

    @pl.when(tp > 0)
    def _():
        greet((seg, seq, tp - 1))

    @pl.when(tp < n_tp - 1)
    def _():
        greet((seg, seq, tp + 1))

    for load in loads:
        load.start()
    table[...] = jnp.zeros(table.shape, table.dtype)
    table[0:1, 0:per_dev] = row_ref[...]
    line = jnp.int32(2) - (tp == 0).astype(jnp.int32) - (tp == n_tp - 1).astype(jnp.int32)
    pl.semaphore_wait(barrier, len(sections) * n_seq + n_seq - 1 + line)

    def remote(src, dst, send, recv, device):
        return pltpu.make_async_remote_copy(
            src_ref=src, dst_ref=dst, send_sem=send, recv_sem=recv,
            device_id=device, device_id_type=MESH,
        )

    pending = []

    own_rows = pl.ds(seq * per_dev, per_dev)
    qy = [
        remote(
            q_hbm.at[:, :, pl.ds(g * part, part)], qbufs[g].at[own_rows],
            qy_send.at[g], qy_recv.at[g], (before, seq, tp),
        )
        for g in range(groups)
    ]
    for copy in qy[:AHEAD]:
        copy.start()
    pending += qy

    tables = [
        remote(table, tbuf.at[seq], t_send.at[m], t_recv.at[m], (after, partner[m], tp))
        for m in range(n_seq)
    ]
    for copy in tables:
        copy.start()
    pending += tables

    steps = hops(n_seq)

    def spread(buf, send, recv, g):
        levels, at = [], 0
        for bit, held in steps:
            level = []
            for mask in held:
                place = buf.at[pl.ds(partner[mask] * per_dev, per_dev)]
                level.append(
                    remote(place, place, send.at[at, g], recv.at[at, g], (seg, partner[bit], tp))
                )
                at += 1
            levels.append(level)
        return levels

    def enter(first, levels):
        first.wait_recv()
        for level in levels:
            level[0].start()

    def relay(levels, depth):
        bit, held = steps[depth]
        for mask, copy in zip(held, levels[depth]):
            copy.wait_recv()
            for later in range(depth + 1, len(steps)):
                levels[later][steps[later][1].index(mask ^ bit)].start()

    q_levels = [spread(qbufs[g], qx_send, qx_recv, g) for g in range(groups)]
    a_levels = [spread(abufs[g], ax_send, ax_recv, g) for g in range(groups)]
    ay = [
        remote(answers[g], abufs[g].at[own_rows], ay_send.at[g], ay_recv.at[g], (after, seq, tp))
        for g in range(groups)
    ]
    pending += [copy for levels in q_levels + a_levels for level in levels for copy in level]
    pending += ay

    position = lax.broadcasted_iota(jnp.int32, (1, span), 1)

    def attend(g):
        if g == 0:
            loads[0].wait()
            loads[1].wait()
        units = [(k, h) for k in range(per_dev) for h in range(part // HD)]
        wide = [pl.ds(g * part + h * HD, HD) for _, h in units]
        valid = []
        for k in range(per_dev):
            limit = jnp.zeros((1, span), jnp.int32)
            for j in range(span // NR):
                inside = (position >= j * NR) & (position < (j + 1) * NR)
                limit = jnp.where(inside, j * NR + len_ref[j, k], limit)
            valid.append(position < limit)
        scores = [
            lax.dot_general(
                qbufs[g][slot_ref[0, k], :, pl.ds(h * HD, HD)], kbuf[k, :, cols],
                (((1,), (1,)), ((), ())), preferred_element_type=F32,
            )
            for (k, h), cols in zip(units, wide)
        ]
        scores = [
            jnp.where(valid[k], one * (1.0 / math.sqrt(HD)), -1e30)
            for (k, _), one in zip(units, scores)
        ]
        highest = [jnp.max(one, axis=1, keepdims=True) for one in scores]
        expo = [jnp.exp(one - top) for one, top in zip(scores, highest)]
        sums = [jnp.sum(one, axis=1, keepdims=True) for one in expo]
        weights = [(one * (1.0 / total)).astype(BF16) for one, total in zip(expo, sums)]
        for (k, h), cols, one in zip(units, wide, weights):
            answers[g][k, :, pl.ds(h * HD, HD)] = jnp.dot(
                one, vbuf[k, :, cols], preferred_element_type=F32
            ).astype(BF16)
        ay[g].start()

    order = list(range(n_seq - 1, -1, -1))
    if ratio == 1:
        mine = lambda c: rbuf.at[seq, c]
    else:
        lanes = pl.ds(pl.multiple_of(lax.rem(seq, ratio) * width, width), width)
        mine = lambda c: rbuf.at[lax.div(seq, ratio), c, :, lanes]
    exchange = {}
    slots = {}

    def find_slots():
        for copy in tables:
            copy.wait_recv()
        scalars = pltpu.make_async_copy(tbuf, tsmem, load_sem.at[4])
        scalars.start()
        scalars.wait()
        served = [tsmem[g // per_dev, 0, g % per_dev] for g in range(n_seq * per_dev)]
        for m in order:
            for c in range(per_dev):
                slot = jnp.int32(0)
                for g, value in enumerate(served):
                    slot = jnp.where(value == partner[m] * per_dev + c, jnp.int32(g), slot)
                slots[m, c] = slot

    def project():
        for k in range(per_dev):
            rows = [
                jnp.concatenate([buf[slots[m, k]] for buf in abufs], axis=1) for m in order
            ]
            product = jnp.dot(
                jnp.concatenate(rows, axis=0), wbuf[...], preferred_element_type=F32
            ).astype(BF16)
            for piece in range(STRETCH // ROWS):
                c = k * (STRETCH // ROWS) + piece
                for at, m in enumerate(order):
                    start = at * STRETCH + piece * ROWS
                    block = product[start:start + ROWS]
                    if m == 0:
                        mine(c)[...] = block
                    else:
                        psend[m - 1, c] = block
                        copy = remote(
                            psend.at[m - 1, c], mine(c), p_send.at[m, c], p_recv.at[seq, c],
                            (seg, partner[m], tp),
                        )
                        copy.start()
                        exchange[m, c] = copy

    depth = len(steps)
    def enter_queries(g):
        enter(qy[g], q_levels[g])
        if g + AHEAD < groups:
            qy[g + AHEAD].start()

    stages = [enter_queries]
    stages += [lambda g, d=d: relay(q_levels[g], d) for d in range(depth)]
    stages[-1] = lambda g: (relay(q_levels[g], depth - 1), attend(g))
    stages += [lambda g: enter(ay[g], a_levels[g])]
    stages += [lambda g, d=d: relay(a_levels[g], d) for d in range(depth)]
    delay = [at + (at > depth) for at in range(len(stages))]
    for turn in range(groups + delay[-1]):
        for stage, late in zip(stages, delay):
            if 0 <= turn - late < groups:
                stage(turn - late)
        if turn == groups:
            find_slots()
    loads[2].wait()
    project()

    last = n_tp - 1

    def arrived(target, c):
        for j in range(ratio):
            origin = target * ratio + j

            @pl.when(origin != seq)
            def _():
                remote(
                    psend.at[0, c], psend.at[0, c], p_send.at[0, c], p_recv.at[origin, c],
                    (seg, partner[1], tp),
                ).wait_recv()

    def along(buf, send, recv, c, target, device):
        place = buf.at[target, c]
        return remote(place, place, send.at[target, c], recv.at[target, c], device)

    def push(buf, send, recv, c, target, first, device):
        @pl.when(first)
        def _():
            buf[target, c] = rbuf[target, c]

        @pl.when(jnp.logical_not(first))
        def _():
            along(buf, send, recv, c, target, device).wait_recv()
            buf[target, c] = (buf[target, c].astype(F32) + rbuf[target, c].astype(F32)).astype(BF16)

        along(buf, send, recv, c, target, device).start()

    def finish(c):
        for buf, send, recv, end, near in (
            (upbuf, up_send, up_recv, 0, -1),
            (downbuf, down_send, down_recv, last, 1),
        ):
            @pl.when(tp == end)
            def _():
                buf[tp, c] = jnp.zeros(buf.shape[2:], buf.dtype)

            @pl.when(tp != end)
            def _():
                along(buf, send, recv, c, tp, (seg, seq, tp + near)).wait_recv()
        own = pl.ds(pl.multiple_of(c * ROWS, ROWS), ROWS)
        total = upbuf[tp, c].astype(F32) + downbuf[tp, c].astype(F32) + rbuf[tp, c].astype(F32)
        out_ref[own, :] = (resbuf[own, :].astype(F32) + total).astype(out_ref.dtype)

    home = lax.div(seq, ratio)
    near = n_tp // 2
    low = home < near
    targets = [jnp.where(low, p, last - p) for p in range(near)]
    targets += [jnp.where(low, last - p, p) for p in range(near)]
    loads[3].wait()

    def each(step, rise, fall):
        for m, target in enumerate(targets):
            begin = step - m // near
            up, down = begin - tp, begin - (last - tp)

            @pl.when((target > tp) & (up >= 0) & (up < chunks))
            def _():
                rise(target, up)

            @pl.when((target < tp) & (down >= 0) & (down < chunks))
            def _():
                fall(target, down)

    def rise(target, c):
        arrived(target, c)
        push(upbuf, up_send, up_recv, c, target, tp == 0, (seg, seq, tp + 1))

    def fall(target, c):
        arrived(target, c)
        push(downbuf, down_send, down_recv, c, target, tp == last, (seg, seq, tp - 1))

    @pl.loop(0, chunks + 1 + last)
    def _(step):
        each(step, rise, fall)
        late = jnp.where(low == (tp < near), 0, 1)
        c = step - jnp.maximum(tp, last - tp) - late

        @pl.when((c >= 0) & (c < chunks))
        def _():
            arrived(tp, c)
            finish(c)

    for copy in pending + list(exchange.values()):
        copy.wait_send()
    @pl.loop(0, chunks + 1 + last)
    def _(step):
        each(
            step,
            lambda target, c: along(
                upbuf, up_send, up_recv, c, target, (seg, seq, tp + 1)
            ).wait_send(),
            lambda target, c: along(
                downbuf, down_send, down_recv, c, target, (seg, seq, tp - 1)
            ).wait_send(),
        )


def local(sizes, queries, nb_keys, nb_values, nb_lengths, slot_stretch, out_weight, residual):
    n_seg, n_seq, n_tp = sizes
    per_dev = slot_stretch.shape[1]
    rows, feats = queries.shape[1:]
    span = nb_keys.shape[2]
    width = out_weight.shape[2]
    keep = residual.shape[2]
    any_spec = pl.BlockSpec(memory_space=pl.ANY)
    smem_spec = pl.BlockSpec(memory_space=pltpu.SMEM)
    vmem_spec = pl.BlockSpec(memory_space=pltpu.VMEM)
    dma = pltpu.SemaphoreType.DMA
    block = (STRETCH, feats // GROUPS)
    chunks = per_dev * STRETCH // ROWS
    mixed = pl.pallas_call(
        functools.partial(kernel, n_seg, n_seq, n_tp, per_dev),
        out_shape=jax.ShapeDtypeStruct((rows, keep), residual.dtype),
        in_specs=[any_spec] * 5 + [smem_spec] * 2 + [vmem_spec],
        out_specs=vmem_spec,
        scratch_shapes=[
            pltpu.VMEM((per_dev, span, feats), BF16),
            pltpu.VMEM((per_dev, span, feats), BF16),
            pltpu.VMEM((feats, width), BF16),
            pltpu.VMEM((rows, keep), BF16),
            [pltpu.VMEM((n_seq * per_dev,) + block, BF16)] * GROUPS,
            [pltpu.VMEM((n_seq * per_dev,) + block, BF16)] * GROUPS,
            [pltpu.VMEM((per_dev,) + block, BF16)] * GROUPS,
            pltpu.VMEM((n_seq - 1, chunks, ROWS, width), BF16),
            pltpu.VMEM((n_tp, chunks, ROWS, keep), BF16),
            pltpu.VMEM((n_tp, chunks, ROWS, keep), BF16),
            pltpu.VMEM((n_tp, chunks, ROWS, keep), BF16),
            pltpu.VMEM((8, 128), jnp.int32),
            pltpu.VMEM((n_seq, 8, 128), jnp.int32),
            pltpu.SMEM((n_seq, 8, 128), jnp.int32),
            dma((5,)),
            dma((GROUPS,)), dma((GROUPS,)),
            dma((n_seq - 1, GROUPS)), dma((n_seq - 1, GROUPS)),
            dma((GROUPS,)), dma((GROUPS,)),
            dma((n_seq - 1, GROUPS)), dma((n_seq - 1, GROUPS)),
            dma((n_seq,)), dma((n_seq,)),
            dma((n_seq, chunks)), dma((n_seq, chunks)),
            dma((n_tp, chunks)), dma((n_tp, chunks)),
            dma((n_tp, chunks)), dma((n_tp, chunks)),
        ],
        compiler_params=pltpu.CompilerParams(
            collective_id=0, has_side_effects=True, vmem_limit_bytes=60 * 1024 * 1024
        ),
    )(
        queries.reshape(per_dev, STRETCH, feats), nb_keys[0], nb_values[0], out_weight[0],
        residual[0], nb_lengths[0].T, slot_stretch, slot_stretch,
    )
    return mixed[None]


def solution(mesh):
    in_specs = (
        P("segment", "seq", "tp"),
        P("segment", "seq", None, "tp"),
        P("segment", "seq", None, "tp"),
        P("segment", "seq", None),
        P("segment", "seq"),
        P("segment", "tp", "seq"),
        P("segment", "seq", "tp"),
    )
    out_specs = P("segment", "seq", "tp")
    sizes = tuple(mesh.shape[name] for name in ("segment", "seq", "tp"))
    return jax.shard_map(
        functools.partial(local, sizes), mesh=mesh, in_specs=in_specs, out_specs=out_specs,
        check_vma=False,
    )
```

```python
import functools
import math

import jax
import jax.numpy as jnp
from jax import lax
from jax.experimental import pallas as pl
from jax.experimental.pallas import tpu as pltpu
from jax.sharding import PartitionSpec as P

HD = 128
STRETCH = 64
NR = 128
GROUPS = 4
ROWS = 16
AHEAD = GROUPS
MESH = pl.DeviceIdType.MESH
F32 = jnp.float32
BF16 = jnp.bfloat16


def hops(count):
    steps, held = [], [0]
    bit = count // 2
    while bit:
        steps.append((bit, tuple(held)))
        held = held + [mask ^ bit for mask in held]
        bit //= 2
    return steps


def kernel(
    n_seg, n_seq, n_tp, per_dev,
    q_hbm, k_hbm, v_hbm, w_hbm, res_hbm, len_ref, slot_ref, row_ref,
    out_ref,
    kbuf, vbuf, wbuf, resbuf, qbufs, abufs, answers, psend, rbuf, upbuf, downbuf, table, tbuf, tsmem,
    load_sem, qy_send, qy_recv, qx_send, qx_recv, ay_send, ay_recv, ax_send, ax_recv,
    t_send, t_recv, p_send, p_recv, up_send, up_recv, down_send, down_recv,
):
    seg, seq, tp = lax.axis_index("segment"), lax.axis_index("seq"), lax.axis_index("tp")
    before = lax.rem(seg + n_seg - 1, n_seg)
    after = lax.rem(seg + 1, n_seg)
    span = k_hbm.shape[1]
    feats = q_hbm.shape[2]
    width = w_hbm.shape[1]
    ratio = n_seq // n_tp
    chunks = per_dev * STRETCH // ROWS
    groups = len(qbufs)
    part = feats // groups

    def xor(mask):
        out, bit = seq, 1
        while bit <= mask:
            if mask & bit:
                digit = lax.rem(lax.div(seq, bit), 2)
                out = out + bit - 2 * bit * digit
            bit *= 2
        return out

    partner = [xor(mask) for mask in range(n_seq)]

    loads = [
        pltpu.make_async_copy(src, dst, load_sem.at[i])
        for i, (src, dst) in enumerate(
            [(k_hbm, kbuf), (v_hbm, vbuf), (w_hbm, wbuf), (res_hbm, resbuf)]
        )
    ]

    barrier = pltpu.get_barrier_semaphore()

    def greet(device):
        pl.semaphore_signal(barrier, inc=1, device_id=device, device_id_type=MESH)

    sections = [after] if n_seg == 2 else [before, after]
    for mask in range(n_seq):
        for section in sections:
            greet((section, partner[mask], tp))
        if mask:
            greet((seg, partner[mask], tp))

    @pl.when(tp > 0)
    def _():
        greet((seg, seq, tp - 1))

    @pl.when(tp < n_tp - 1)
    def _():
        greet((seg, seq, tp + 1))

    for load in loads:
        load.start()
    table[...] = jnp.zeros(table.shape, table.dtype)
    table[0:1, 0:per_dev] = row_ref[...]
    line = jnp.int32(2) - (tp == 0).astype(jnp.int32) - (tp == n_tp - 1).astype(jnp.int32)
    pl.semaphore_wait(barrier, len(sections) * n_seq + n_seq - 1 + line)

    def remote(src, dst, send, recv, device):
        return pltpu.make_async_remote_copy(
            src_ref=src, dst_ref=dst, send_sem=send, recv_sem=recv,
            device_id=device, device_id_type=MESH,
        )

    pending = []

    own_rows = pl.ds(seq * per_dev, per_dev)
    qy = [
        remote(
            q_hbm.at[:, :, pl.ds(g * part, part)], qbufs[g].at[own_rows],
            qy_send.at[g], qy_recv.at[g], (before, seq, tp),
        )
        for g in range(groups)
    ]
    for copy in qy[:AHEAD]:
        copy.start()
    pending += qy

    tables = [
        remote(table, tbuf.at[seq], t_send.at[m], t_recv.at[m], (after, partner[m], tp))
        for m in range(n_seq)
    ]
    for copy in tables:
        copy.start()
    pending += tables

    steps = hops(n_seq)

    def spread(buf, send, recv, g):
        levels, at = [], 0
        for bit, held in steps:
            level = []
            for mask in held:
                place = buf.at[pl.ds(partner[mask] * per_dev, per_dev)]
                level.append(
                    remote(place, place, send.at[at, g], recv.at[at, g], (seg, partner[bit], tp))
                )
                at += 1
            levels.append(level)
        return levels

    def enter(first, levels):
        first.wait_recv()
        for level in levels:
            level[0].start()

    def relay(levels, depth):
        bit, held = steps[depth]
        for mask, copy in zip(held, levels[depth]):
            copy.wait_recv()
            for later in range(depth + 1, len(steps)):
                levels[later][steps[later][1].index(mask ^ bit)].start()

    q_levels = [spread(qbufs[g], qx_send, qx_recv, g) for g in range(groups)]
    a_levels = [spread(abufs[g], ax_send, ax_recv, g) for g in range(groups)]
    ay = [
        remote(answers[g], abufs[g].at[own_rows], ay_send.at[g], ay_recv.at[g], (after, seq, tp))
        for g in range(groups)
    ]
    pending += [copy for levels in q_levels + a_levels for level in levels for copy in level]
    pending += ay

    position = lax.broadcasted_iota(jnp.int32, (1, span), 1)

    def attend(g):
        if g == 0:
            loads[0].wait()
            loads[1].wait()
        units = [(k, h) for k in range(per_dev) for h in range(part // HD)]
        wide = [pl.ds(g * part + h * HD, HD) for _, h in units]
        valid = []
        for k in range(per_dev):
            limit = jnp.zeros((1, span), jnp.int32)
            for j in range(span // NR):
                inside = (position >= j * NR) & (position < (j + 1) * NR)
                limit = jnp.where(inside, j * NR + len_ref[j, k], limit)
            valid.append(position < limit)
        scores = [
            lax.dot_general(
                qbufs[g][slot_ref[0, k], :, pl.ds(h * HD, HD)], kbuf[k, :, cols],
                (((1,), (1,)), ((), ())), preferred_element_type=F32,
            )
            for (k, h), cols in zip(units, wide)
        ]
        scores = [
            jnp.where(valid[k], one * (1.0 / math.sqrt(HD)), -1e30)
            for (k, _), one in zip(units, scores)
        ]
        highest = [jnp.max(one, axis=1, keepdims=True) for one in scores]
        expo = [jnp.exp(one - top) for one, top in zip(scores, highest)]
        sums = [jnp.sum(one, axis=1, keepdims=True) for one in expo]
        weights = [(one * (1.0 / total)).astype(BF16) for one, total in zip(expo, sums)]
        for (k, h), cols, one in zip(units, wide, weights):
            answers[g][k, :, pl.ds(h * HD, HD)] = jnp.dot(
                one, vbuf[k, :, cols], preferred_element_type=F32
            ).astype(BF16)
        ay[g].start()

    order = list(range(n_seq - 1, -1, -1))
    if ratio == 1:
        mine = lambda c: rbuf.at[seq, c]
    else:
        lanes = pl.ds(pl.multiple_of(lax.rem(seq, ratio) * width, width), width)
        mine = lambda c: rbuf.at[lax.div(seq, ratio), c, :, lanes]
    exchange = {}
    slots = {}

    def find_slots():
        for copy in tables:
            copy.wait_recv()
        scalars = pltpu.make_async_copy(tbuf, tsmem, load_sem.at[4])
        scalars.start()
        scalars.wait()
        served = [tsmem[g // per_dev, 0, g % per_dev] for g in range(n_seq * per_dev)]
        for m in order:
            for c in range(per_dev):
                slot = jnp.int32(0)
                for g, value in enumerate(served):
                    slot = jnp.where(value == partner[m] * per_dev + c, jnp.int32(g), slot)
                slots[m, c] = slot

    def project():
        for k in range(per_dev):
            rows = [
                jnp.concatenate([buf[slots[m, k]] for buf in abufs], axis=1) for m in order
            ]
            product = jnp.dot(
                jnp.concatenate(rows, axis=0), wbuf[...], preferred_element_type=F32
            ).astype(BF16)
            for piece in range(STRETCH // ROWS):
                c = k * (STRETCH // ROWS) + piece
                for at, m in enumerate(order):
                    start = at * STRETCH + piece * ROWS
                    block = product[start:start + ROWS]
                    if m == 0:
                        mine(c)[...] = block
                    else:
                        psend[m - 1, c] = block
                        copy = remote(
                            psend.at[m - 1, c], mine(c), p_send.at[m, c], p_recv.at[seq, c],
                            (seg, partner[m], tp),
                        )
                        copy.start()
                        exchange[m, c] = copy

    depth = len(steps)
    def enter_queries(g):
        enter(qy[g], q_levels[g])
        if g + AHEAD < groups:
            qy[g + AHEAD].start()

    stages = [enter_queries]
    stages += [lambda g, d=d: relay(q_levels[g], d) for d in range(depth)]
    stages[-1] = lambda g: (relay(q_levels[g], depth - 1), attend(g))
    stages += [lambda g: enter(ay[g], a_levels[g])]
    stages += [lambda g, d=d: relay(a_levels[g], d) for d in range(depth)]
    delay = [at + (at > depth) for at in range(len(stages))]
    for turn in range(groups + delay[-1]):
        for stage, late in zip(stages, delay):
            if 0 <= turn - late < groups:
                stage(turn - late)
        if turn == groups:
            find_slots()
    loads[2].wait()
    project()

    last = n_tp - 1

    def arrived(target, c):
        for j in range(ratio):
            origin = target * ratio + j

            @pl.when(origin != seq)
            def _():
                remote(
                    psend.at[0, c], psend.at[0, c], p_send.at[0, c], p_recv.at[origin, c],
                    (seg, partner[1], tp),
                ).wait_recv()

    def along(buf, send, recv, c, target, device):
        place = buf.at[target, c]
        return remote(place, place, send.at[target, c], recv.at[target, c], device)

    def push(buf, send, recv, c, target, first, device):
        @pl.when(first)
        def _():
            buf[target, c] = rbuf[target, c]

        @pl.when(jnp.logical_not(first))
        def _():
            along(buf, send, recv, c, target, device).wait_recv()
            buf[target, c] = (buf[target, c].astype(F32) + rbuf[target, c].astype(F32)).astype(BF16)

        along(buf, send, recv, c, target, device).start()

    def finish(c):
        for buf, send, recv, end, near in (
            (upbuf, up_send, up_recv, 0, -1),
            (downbuf, down_send, down_recv, last, 1),
        ):
            @pl.when(tp == end)
            def _():
                buf[tp, c] = jnp.zeros(buf.shape[2:], buf.dtype)

            @pl.when(tp != end)
            def _():
                along(buf, send, recv, c, tp, (seg, seq, tp + near)).wait_recv()
        own = pl.ds(pl.multiple_of(c * ROWS, ROWS), ROWS)
        total = upbuf[tp, c].astype(F32) + downbuf[tp, c].astype(F32) + rbuf[tp, c].astype(F32)
        out_ref[own, :] = (resbuf[own, :].astype(F32) + total).astype(out_ref.dtype)

    home = lax.div(seq, ratio)
    near = n_tp // 2
    low = home < near
    targets = [jnp.where(low, p, last - p) for p in range(near)]
    targets += [jnp.where(low, last - p, p) for p in range(near)]
    loads[3].wait()

    def each(step, rise, fall):
        for m, target in enumerate(targets):
            begin = step - m // near
            up, down = begin - tp, begin - (last - tp)

            @pl.when((target > tp) & (up >= 0) & (up < chunks))
            def _():
                rise(target, up)

            @pl.when((target < tp) & (down >= 0) & (down < chunks))
            def _():
                fall(target, down)

    def rise(target, c):
        arrived(target, c)
        push(upbuf, up_send, up_recv, c, target, tp == 0, (seg, seq, tp + 1))

    def fall(target, c):
        arrived(target, c)
        push(downbuf, down_send, down_recv, c, target, tp == last, (seg, seq, tp - 1))

    @pl.loop(0, chunks + 1 + last)
    def _(step):
        each(step, rise, fall)
        late = jnp.where(low == (tp < near), 0, 1)
        c = step - jnp.maximum(tp, last - tp) - late

        @pl.when((c >= 0) & (c < chunks))
        def _():
            arrived(tp, c)
            finish(c)

    for copy in pending + list(exchange.values()):
        copy.wait_send()
    @pl.loop(0, chunks + 1 + last)
    def _(step):
        each(
            step,
            lambda target, c: along(
                upbuf, up_send, up_recv, c, target, (seg, seq, tp + 1)
            ).wait_send(),
            lambda target, c: along(
                downbuf, down_send, down_recv, c, target, (seg, seq, tp - 1)
            ).wait_send(),
        )


def local(sizes, queries, nb_keys, nb_values, nb_lengths, slot_stretch, out_weight, residual):
    n_seg, n_seq, n_tp = sizes
    per_dev = slot_stretch.shape[1]
    rows, feats = queries.shape[1:]
    span = nb_keys.shape[2]
    width = out_weight.shape[2]
    keep = residual.shape[2]
    any_spec = pl.BlockSpec(memory_space=pl.ANY)
    smem_spec = pl.BlockSpec(memory_space=pltpu.SMEM)
    vmem_spec = pl.BlockSpec(memory_space=pltpu.VMEM)
    dma = pltpu.SemaphoreType.DMA
    block = (STRETCH, feats // GROUPS)
    chunks = per_dev * STRETCH // ROWS
    mixed = pl.pallas_call(
        functools.partial(kernel, n_seg, n_seq, n_tp, per_dev),
        out_shape=jax.ShapeDtypeStruct((rows, keep), residual.dtype),
        in_specs=[any_spec] * 5 + [smem_spec] * 2 + [vmem_spec],
        out_specs=vmem_spec,
        scratch_shapes=[
            pltpu.VMEM((per_dev, span, feats), BF16),
            pltpu.VMEM((per_dev, span, feats), BF16),
            pltpu.VMEM((feats, width), BF16),
            pltpu.VMEM((rows, keep), BF16),
            [pltpu.VMEM((n_seq * per_dev,) + block, BF16)] * GROUPS,
            [pltpu.VMEM((n_seq * per_dev,) + block, BF16)] * GROUPS,
            [pltpu.VMEM((per_dev,) + block, BF16)] * GROUPS,
            pltpu.VMEM((n_seq - 1, chunks, ROWS, width), BF16),
            pltpu.VMEM((n_tp, chunks, ROWS, keep), BF16),
            pltpu.VMEM((n_tp, chunks, ROWS, keep), BF16),
            pltpu.VMEM((n_tp, chunks, ROWS, keep), BF16),
            pltpu.VMEM((8, 128), jnp.int32),
            pltpu.VMEM((n_seq, 8, 128), jnp.int32),
            pltpu.SMEM((n_seq, 8, 128), jnp.int32),
            dma((5,)),
            dma((GROUPS,)), dma((GROUPS,)),
            dma((n_seq - 1, GROUPS)), dma((n_seq - 1, GROUPS)),
            dma((GROUPS,)), dma((GROUPS,)),
            dma((n_seq - 1, GROUPS)), dma((n_seq - 1, GROUPS)),
            dma((n_seq,)), dma((n_seq,)),
            dma((n_seq, chunks)), dma((n_seq, chunks)),
            dma((n_tp, chunks)), dma((n_tp, chunks)),
            dma((n_tp, chunks)), dma((n_tp, chunks)),
        ],
        compiler_params=pltpu.CompilerParams(
            collective_id=0, has_side_effects=True, vmem_limit_bytes=60 * 1024 * 1024
        ),
    )(
        queries.reshape(per_dev, STRETCH, feats), nb_keys[0], nb_values[0], out_weight[0],
        residual[0], nb_lengths[0].T, slot_stretch, slot_stretch,
    )
    return mixed[None]


def solution(mesh):
    in_specs = (
        P("segment", "seq", "tp"),
        P("segment", "seq", None, "tp"),
        P("segment", "seq", None, "tp"),
        P("segment", "seq", None),
        P("segment", "seq"),
        P("segment", "tp", "seq"),
        P("segment", "seq", "tp"),
    )
    out_specs = P("segment", "seq", "tp")
    sizes = tuple(mesh.shape[name] for name in ("segment", "seq", "tp"))
    return jax.shard_map(
        functools.partial(local, sizes), mesh=mesh, in_specs=in_specs, out_specs=out_specs,
        check_vma=False,
    )
```
